512 devices in a mesh: dp: 32 (over y_hi, x, core), blk: 16 (over z, y_lo).
Axes of the slice: x: 4, y: 8 (y_hi: 4, y_lo: 2; y = y_hi * 2 + y_lo), z: 8, core: 2. Of those that a mesh axis runs over, the one named last changes fastest.
Arguments:
- points: bfloat16 [32768, 1024], P(('dp', 'blk')), may hold values from -6 to 6
- membership: int32 [32768], P(('dp', 'blk')), may hold values from 0 to 511
- landmark_pool: bfloat16 [12288, 1024], P('blk'), may hold values from -6 to 6
- landmark_ids: int32 [8192], P('blk'), may hold values from 0 to 767, as said below
- whitening: bfloat16 [8192, 1024], P('blk'), may hold values from -0.03125 to 0.03125
- owner_map: int32 [512], replicated, may hold values from 0 to 31, as said below
Outputs:
- features: bfloat16 [32768, 1024], P(('dp', 'blk'))
- owned_centroids: bfloat16 [512, 1024], P('dp')
- scores: float32 [32768, 512], P(('dp', 'blk'))
The draws below stay inside these ranges and needn't reach their ends.
Inputs may be any that keep to these rules, and one draw needn't show every extreme that they name: `landmark_ids`: id i of landmark block b names row b * 768 + i of landmark_pool; the first id of every block is 0 and the last is 767. `owner_map`: every owner is named by exactly 16 clusters.
All inputs are finite; a program needn't handle non-finite values.
Results may differ from the reference program's by a relative error of at most 0.015.
Values may be sent and summed in bfloat16 or wider, within the bound.
No kernel may reach another device: no remote copies, remote signals or barrier semaphores. Data moves between devices by JAX's collectives and lax.ppermute only.
A program may use at most 64 MiB of HBM per device.

```python
import math
import jax
import jax.numpy as jnp
from jax import lax

VECTOR_EXTENT = 1024
R = 1024
M = 8192
C = 512
POINTS = 32768
MB = 512
POOL_DEV = 768
CPO = 16
N_BLK = 16


def draw_membership(key, part):
    key = jax.random.fold_in(key, 5)
    first, second, third, fourth = jax.random.split(key, 4)
    upper = jax.random.randint(first, (POINTS,), 0, C)
    lower = jax.random.randint(second, (POINTS,), 0, C)
    ranked = upper * lower // C
    shuffled = jax.random.permutation(third, C).astype(jnp.int32)
    labels = shuffled[ranked]
    vacant = jax.random.permutation(fourth, C - 2)[:8].astype(jnp.int32) + 1
    taken = jnp.any(labels[:, None] == vacant[None, :], axis=1)
    labels = jnp.where(taken, 0, labels)
    position = jnp.arange(POINTS)
    labels = jnp.where(position == 0, 0, jnp.where(position == POINTS - 1, C - 1, labels))
    return labels.astype(jnp.int32)


def draw_landmark_ids(key, part):
    key = jax.random.fold_in(key, 7)
    chosen = jax.random.randint(key, (M,), 0, POOL_DEV)
    position = jnp.arange(M) % MB
    chosen = jnp.where(position == 0, 0, jnp.where(position == MB - 1, POOL_DEV - 1, chosen))
    return chosen.astype(jnp.int32)


def draw_owner_map(key, part):
    key = jax.random.fold_in(key, 11)
    shuffled = jax.random.permutation(key, C)
    return (shuffled // CPO).astype(jnp.int32)


def shard_levels(own_key, dims, shards, low, high):
    gain, own = 1.0, jax.random.fold_in(own_key, 6)
    for dim, blocks in shards:
        steps = jnp.exp(jax.random.uniform(jax.random.fold_in(own, dim), (blocks,), jnp.float32, low / len(shards), high / len(shards)))
        gain = gain * jnp.repeat(steps, dims[dim] // blocks).reshape([-1 if axis == dim else 1 for axis in range(len(dims))])
    return gain


def scatter_about(rng, extent, scale, limit, cuts=(), dtype=jnp.bfloat16):
    level = shard_levels(rng, extent, cuts, -0.22, 0.18) if cuts else 1.0
    entries = jax.random.normal(rng, extent, jnp.float32) * scale * level
    return jnp.minimum(jnp.maximum(entries, -limit), limit).astype(dtype)


def setup_inputs(seed: int = 0) -> dict:
    seeds = jax.random.split(jax.random.key(seed), 7)
    return {
        "points": scatter_about(seeds[0], (POINTS, VECTOR_EXTENT), 1.0, 6.0, ((0, 512),)),
        "membership": draw_membership(jax.random.fold_in(seeds[6], 71), 0),
        "landmark_pool": scatter_about(seeds[2], (N_BLK * POOL_DEV, VECTOR_EXTENT), 1.0, 6.0, ((0, 16),)),
        "landmark_ids": draw_landmark_ids(jax.random.fold_in(seeds[6], 71), 0),
        "whitening": scatter_about(seeds[4], (M, R), (4 * M) ** -0.5, 0.03125, ((0, 16),)),
        "owner_map": draw_owner_map(jax.random.fold_in(seeds[6], 71), 0),
    }


epsilon = 1e-06

def reference(points, membership, landmark_pool, landmark_ids, whitening, owner_map):
    chosen = (jnp.arange(M) // MB).astype(jnp.int32) * POOL_DEV + landmark_ids.astype(jnp.int32)
    landmarks = landmark_pool[chosen]
    anchor_magnitude_factor = lax.rsqrt(lax.optimization_barrier(jnp.sum(jnp.square(landmarks.astype(jnp.float32)), axis=1)) + epsilon)
    softness_divisor = math.sqrt(VECTOR_EXTENT)
    block = min(512, POINTS)

    def featurize(rows_block):
        sample_anchor_gram = jnp.dot(rows_block, landmarks.T, preferred_element_type=jnp.float32)
        sample_length_factor = lax.rsqrt(lax.optimization_barrier(jnp.sum(jnp.square(rows_block.astype(jnp.float32)), axis=1)) + epsilon)
        angular_affinity = softness_divisor * sample_anchor_gram * sample_length_factor[:, None] * anchor_magnitude_factor[None, :]
        kernel = jnp.exp(angular_affinity).astype(jnp.bfloat16)
        return jnp.dot(kernel, whitening, preferred_element_type=jnp.float32).astype(jnp.bfloat16)
    features = lax.map(featurize, points.reshape(POINTS // block, block, VECTOR_EXTENT)).reshape(POINTS, R)
    totals = jax.ops.segment_sum(features.astype(jnp.float32), membership, num_segments=C)
    counts = jax.ops.segment_sum(jnp.ones((POINTS,), jnp.float32), membership, num_segments=C)
    centroids = (totals / jnp.maximum(counts, 1.0)[:, None]).astype(jnp.bfloat16)
    ordering = jnp.argsort(owner_map, stable=True)
    owned_centroids = centroids[ordering]
    centre_f = centroids.astype(jnp.float32)
    squared_norms = lax.optimization_barrier(jnp.sum(centre_f * centre_f, axis=1))
    inner = jnp.dot(features, centroids.T, preferred_element_type=jnp.float32)
    scores = (squared_norms[None, :] - 2.0 * inner) / R
    return (features, owned_centroids, scores)
```

```python
import math

import jax
import jax.numpy as jnp
from jax import lax
from jax.sharding import Mesh, PartitionSpec as P

epsilon = 1e-06
bf16 = jnp.bfloat16
f32 = jnp.float32
ALL = ("yh", "x", "c", "z", "yl")
PLANE = ("yh", "x", "yl")
PACK = 16


def hop(value, axis, by):
    size = math.prod(lax.axis_size(name) for name in (axis if isinstance(axis, tuple) else (axis,)))
    return lax.ppermute(value, axis, [(i, (i + by) % size) for i in range(size)])


def flip(value, axis, bit):
    size = lax.axis_size(axis)
    return lax.ppermute(value, axis, [(i, i ^ bit) for i in range(size)])


def pick(matrix, start, count):
    return lax.dynamic_slice_in_dim(matrix, start, count, 0)


def ordered(mine, other, first):
    return jnp.where(first, jnp.concatenate([mine, other]), jnp.concatenate([other, mine]))


def body(points, membership, landmark_pool, landmark_ids, whitening, owner_map):
    rows, width = points.shape
    rank_width = whitening.shape[1]
    clusters = owner_map.shape[0]
    ring = lax.axis_size("z")
    core = lax.axis_index("c")
    first = core == 0
    upper = lax.axis_index("yl") == 0
    quarter = landmark_ids.shape[0] // 4

    digits = jnp.stack([membership // 128, membership % 128]).astype(bf16)
    tail = jnp.zeros((PACK, width), bf16).at[:2, :rows].set(digits)
    block = jnp.concatenate([points, tail])

    landmarks = landmark_pool[landmark_ids]

    def exchange(matrix):
        up = hop(pick(matrix, 2 * core * quarter, quarter), ("yh", "yl"), 1)
        down = hop(pick(matrix, (2 * core + 1) * quarter, quarter), ("yh", "yl"), -1)
        mine = jnp.concatenate([up, down])
        return ordered(mine, flip(mine, "c", 1), first)

    ahead, behind = [block], [block]
    partner = None
    for step in range(ring // 2):
        ahead.append(hop(ahead[-1], "z", 1))
        if step < ring // 2 - 1:
            behind.append(hop(behind[-1], "z", -1))
    partner = exchange(landmarks)
    partner_white = exchange(whitening)
    offsets = [-k for k in range(ring // 2 + 1)] + list(range(1, ring // 2))
    held = ahead + behind[1:]
    visitors = jnp.concatenate([part[:rows] for part in held])
    codes = jnp.stack([part[rows : rows + 2, :rows] for part in held], 1).reshape(2, ring * rows)
    members = codes[0].astype(jnp.int32) * 128 + codes[1].astype(jnp.int32)

    def inverse_length(matrix):
        return lax.rsqrt(jnp.sum(jnp.square(matrix.astype(f32)), axis=1) + epsilon)

    visitor_factor = inverse_length(visitors) * math.sqrt(width)

    def affinity(anchors):
        gram = lax.dot_general(visitors, anchors, (((1,), (1,)), ((), ())), preferred_element_type=f32)
        return jnp.exp(gram * visitor_factor[:, None] * inverse_length(anchors)[None, :]).astype(bf16)

    kernel_own = affinity(landmarks)
    kernel_partner = affinity(partner)
    table = jnp.arange(clusters, dtype=jnp.int32)[:, None] == members[None, :]
    counted = jnp.sum(table.astype(jnp.int32), axis=1)
    table = table.astype(bf16)
    sums_own = jnp.dot(table, kernel_own, preferred_element_type=f32).astype(bf16)
    sums_partner = jnp.dot(table, kernel_partner, preferred_element_type=f32).astype(bf16)
    count_tail = (
        jnp.zeros((clusters, 128), bf16)
        .at[:, 0].set((counted // 128).astype(bf16))
        .at[:, 1].set((counted % 128).astype(bf16))
    )
    sums = jnp.concatenate(
        [jnp.where(upper, sums_own, sums_partner), jnp.where(upper, sums_partner, sums_own), count_tail], 1
    )
    half = clusters // 2
    theirs = flip(pick(sums, (1 - core) * half, half), "c", 1)
    paired = (pick(sums, core * half, half).astype(f32) + theirs.astype(f32)).astype(bf16)
    peers = math.prod(lax.axis_size(name) for name in PLANE)
    share = half // peers

    partial = (
        jnp.dot(kernel_own, whitening, preferred_element_type=f32)
        + jnp.dot(kernel_partner, partner_white, preferred_element_type=f32)
    ).reshape(ring, rows, rank_width)
    place = {off: partial[i] for i, off in enumerate(offsets)}
    place[ring // 2] = place[-(ring // 2)]
    plus = place[ring // 2].astype(bf16)
    minus = place[-(ring // 2 - 1)].astype(bf16)
    for k in range(ring // 2 - 1, -1, -1):
        plus = hop(plus, "z", 1).astype(f32) + (place[k] if k else 0.0)
        if k:
            plus = plus.astype(bf16)
        if k < ring // 2 - 1:
            minus = hop(minus, "z", -1).astype(f32) + (place[-k] if k else 0.0)
            if k:
                minus = minus.astype(bf16)
    features = (place[0] + plus + minus).astype(bf16)

    spread = lax.all_to_all(paired.reshape(peers, share, -1), PLANE, 0, 0)
    total = jnp.sum(spread.astype(f32), axis=0)
    sums_f = total[:, : 2 * landmark_ids.shape[0]]
    high = sums_f.astype(bf16)
    low = (sums_f - high.astype(f32)).astype(bf16)
    white = jnp.where(upper, jnp.concatenate([whitening, partner_white]), jnp.concatenate([partner_white, whitening]))
    mapped = jnp.dot(jnp.concatenate([high, low]), white, preferred_element_type=f32)
    mapped = mapped[:share] + mapped[share:]
    number = total[:, -128] * 128.0 + total[:, -127]
    bit = 1
    while bit < ring:
        mapped = mapped + flip(mapped, "z", bit)
        bit *= 2
    means = (mapped / jnp.maximum(number, 1.0)[:, None]).astype(bf16)

    sent = jnp.broadcast_to(means[None], (peers, share, rank_width))
    mine = lax.all_to_all(sent, PLANE, 0, 0).reshape(half, rank_width)
    other = flip(mine, "c", 1)
    centroids = ordered(mine, other, first)

    owner = lax.axis_index(("yh", "x", "c"))
    owned_by = (owner_map == owner).astype(jnp.int32)
    slot = jnp.cumsum(owned_by) - 1
    per_owner = clusters // (lax.axis_size("yh") * lax.axis_size("x") * lax.axis_size("c"))
    choose = (jnp.arange(per_owner)[:, None] == slot[None, :]) & (owned_by[None, :] == 1)
    owned_centroids = jnp.dot(choose.astype(bf16), centroids, preferred_element_type=f32).astype(bf16)

    centre = centroids.astype(f32)
    squared_norms = jnp.sum(centre * centre, axis=1)
    inner = lax.dot_general(features, centroids, (((1,), (1,)), ((), ())), preferred_element_type=f32)
    scores = (squared_norms[None, :] - 2.0 * inner) / rank_width
    return (features, owned_centroids, scores)


def build(mesh, factors):
    fine = Mesh(mesh.devices.reshape(factors), ALL)
    blk, dp = ("z", "yl"), ("yh", "x", "c")
    return jax.shard_map(
        body,
        mesh=fine,
        in_specs=(P(ALL, None), P(ALL), P(blk, None), P(blk), P(blk, None), P()),
        out_specs=(P(ALL, None), P(dp, None), P(ALL, None)),
        check_vma=False,
    )


def solution(mesh):
    return build(mesh, (4, 4, 2, 8, 2))
```

```python
import functools
import math

import jax
import jax.numpy as jnp
from jax import lax
from jax.experimental import pallas as pl
from jax.experimental.pallas import tpu as pltpu
from jax.sharding import Mesh, PartitionSpec as P

epsilon = 1e-06
bf16 = jnp.bfloat16
f32 = jnp.float32
i32 = jnp.int32
ALL = ("yh", "x", "c", "z", "yl")
PLANE = ("yh", "x", "yl")
PACK = 16
DIGIT = 128
TALLY = 128
MIB = 1 << 20


def hop(value, axis, by):
    size = math.prod(lax.axis_size(name) for name in axis)
    return lax.ppermute(value, axis, [(i, (i + by) % size) for i in range(size)])


def flip(value, axis, bit):
    size = lax.axis_size(axis)
    return lax.ppermute(value, axis, [(i, i ^ bit) for i in range(size)])


def across(a, b):
    return lax.dot_general(a, b, (((1,), (1,)), ((), ())), preferred_element_type=f32)


def call(kernel, out, ins, scratch=(), flops=0, nbytes=0):
    spec = pl.BlockSpec(memory_space=pltpu.VMEM)
    return pl.pallas_call(
        kernel,
        out_shape=out,
        in_specs=[pl.BlockSpec(memory_space=pltpu.SMEM)] + [spec] * (ins - 1),
        out_specs=jax.tree.map(lambda _: spec, out),
        scratch_shapes=list(scratch),
        compiler_params=pltpu.CompilerParams(vmem_limit_bytes=24 * MIB),
        cost_estimate=pl.CostEstimate(flops=flops, bytes_accessed=nbytes, transcendentals=0),
    )


def row_squares(matrix):
    square = jnp.square(matrix.astype(f32))
    high = square.astype(bf16)
    low = (square - high.astype(f32)).astype(bf16)
    ones = jnp.ones((8, matrix.shape[1]), bf16)
    return across(ones, high) + across(ones, low)


def prepare_kernel(place, own, white, up, down, up_o, down_o, anchors, maps, factor):
    core, half = place[0], place[1]
    count = own.shape[0]
    quarter = count // 4
    mine = pl.multiple_of(half * count, count)
    anchors[pl.ds(mine, count), :] = own[...]
    maps[pl.ds(mine, count), :] = white[...]
    base = (1 - half) * count
    for piece, first, second in ((0, up, up_o), (1, down, down_o)):
        for source, which in ((first, core), (second, 1 - core)):
            at = pl.multiple_of(base + (2 * which + piece) * quarter, quarter)
            anchors[pl.ds(at, quarter), :] = source[:quarter, :]
            maps[pl.ds(at, quarter), :] = source[quarter:, :]
    tile = min(256, count)

    @pl.loop(0, 2 * count // tile)
    def _(j):
        at = pl.multiple_of(j * tile, tile)
        factor[:, pl.ds(at, tile)] = lax.rsqrt(row_squares(anchors[pl.ds(at, tile), :]) + epsilon)


def affinity_kernel(rows, place, spread, anchors, factor, kernel, keep, send, table):
    core, level = place[0], place[3]
    ring, _, width = spread.shape
    half = keep.shape[0]
    count = anchors.shape[0]
    points = ring * rows
    codes = jnp.sum(spread[:, rows:, :].astype(f32), axis=0)
    members = (codes[0:1, :points] * DIGIT + codes[1:2, :points]).astype(i32)
    label = lax.broadcasted_iota(i32, (half, points), 0)
    for ref, part in ((keep, 0), (send, 1)):
        which = jnp.where(core == 0, part, 1 - part)
        hit = jnp.where(label + which * half == members, 1.0, 0.0)
        table[part * half : (part + 1) * half, :] = hit.astype(bf16)
        tally = jnp.sum(hit, axis=1, keepdims=True)
        big = jnp.floor(tally * (1.0 / DIGIT))
        lane = lax.broadcasted_iota(i32, (half, TALLY), 1)
        digits = jnp.where(lane == 0, big, jnp.where(lane == 1, tally - big * DIGIT, 0.0))
        ref[:, count:] = digits.astype(bf16)
    visitors = spread[:, :rows, :].reshape(points, width)
    length = lax.rsqrt(jnp.sum(jnp.square(visitors.astype(f32)), axis=1, keepdims=True) + epsilon) * math.sqrt(width)
    tile = min(256, count)

    @pl.loop(0, count // tile)
    def _(j):
        at = pl.multiple_of(j * tile, tile)
        values = spread[:, :rows, :].reshape(points, width)
        gram = across(values, anchors[pl.ds(at, tile), :])
        part = jnp.exp(gram * length * factor[0:1, pl.ds(at, tile)]).astype(bf16)
        for b in range(ring):
            to = pl.multiple_of(lax.rem(b - level + ring, ring) * rows, rows)
            kernel[pl.ds(to, rows), pl.ds(at, tile)] = part[b * rows : (b + 1) * rows]
        sums = jnp.dot(table[...], part, preferred_element_type=f32).astype(bf16)
        keep[:, pl.ds(at, tile)] = sums[:half]
        send[:, pl.ds(at, tile)] = sums[half:]


def project_kernel(first, place, kernel, maps, *rest):
    outs = [ref for ref in rest if ref.shape[0] == rest[-1].shape[0]]
    rows, width = outs[0].shape
    tile = min(256, width)

    @pl.loop(0, width // tile)
    def _(j):
        at = pl.multiple_of(j * tile, tile)
        span = kernel[first * rows : (first + len(outs)) * rows, :]
        part = jnp.dot(span, maps[:, pl.ds(at, tile)], preferred_element_type=f32)
        for i, out in enumerate(outs):
            out[:, pl.ds(at, tile)] = part[i * rows : (i + 1) * rows].astype(out.dtype)


def cluster_kernel(place, spread, maps, *rest):
    mapped, number = rest[-2:]
    count = maps.shape[0]
    share = spread.shape[1]
    total = jnp.sum(spread[...].astype(f32), axis=0)
    sums = total[:, :count]
    high = sums.astype(bf16).astype(f32)
    both = jnp.concatenate([high, sums - high]).astype(bf16)
    width = maps.shape[1]
    tile = min(256, width)

    result = jnp.dot(both, maps[...], preferred_element_type=f32)
    mapped[...] = result[:share] + result[share:]
    tally = total[:, count : count + 1] * DIGIT + total[:, count + 1 : count + 2]
    number[...] = jnp.broadcast_to(jnp.maximum(tally, 1.0), number.shape)


def feature_kernel(place, owners, *rest):
    arrived, *parts, features, choose, means = rest
    means[...] = arrived[...]
    features[...] = functools.reduce(jnp.add, [part[...].astype(f32) for part in parts]).astype(bf16)
    slots, clusters = choose.shape
    owned = owners[...] == place[2]
    row = lax.broadcasted_iota(i32, (clusters, clusters), 0)
    col = lax.broadcasted_iota(i32, (clusters, clusters), 1)
    before = jnp.where(row < col, 1.0, 0.0).astype(bf16)
    mark = jnp.broadcast_to(jnp.where(owned, 1.0, 0.0), (slots, clusters))
    rank = jnp.dot(mark.astype(bf16), before, preferred_element_type=f32)
    slot = lax.broadcasted_iota(i32, (slots, clusters), 0).astype(f32)
    choose[...] = jnp.where(rank == slot, mark, 0.0).astype(bf16)


def half_scores(features, means, choose, at):
    half = means.shape[0]
    norms = row_squares(means[...])[0:1]
    scores = (norms - 2.0 * across(features[...], means[...])) * (1.0 / means.shape[1])
    owned = jnp.dot(choose[:, pl.ds(at, half)], means[...], preferred_element_type=f32)
    return scores, owned


def near_kernel(place, features, means, choose, scores, owned):
    half = means.shape[0]
    at = pl.multiple_of(place[0] * half, half)
    scores[...], owned[...] = half_scores(features, means, choose, at)


def far_kernel(place, features, means, choose, near_scores, near_owned, scores, owned):
    half = means.shape[0]
    there = pl.multiple_of((1 - place[0]) * half, half)
    here = pl.multiple_of(place[0] * half, half)
    far, rest = half_scores(features, means, choose, there)
    scores[:, pl.ds(there, half)] = far
    scores[:, pl.ds(here, half)] = near_scores[...]
    owned[...] = (near_owned[...] + rest).astype(bf16)


def body(points, membership, landmark_pool, landmark_ids, whitening, owner_map):
    rows, width = points.shape
    count, rank_width = whitening.shape
    clusters = owner_map.shape[0]
    ring = lax.axis_size("z")
    core = lax.axis_index("c")
    quarter = count // 4
    half = clusters // 2
    peers = math.prod(lax.axis_size(name) for name in PLANE)
    share = half // peers
    groups = lax.axis_size("yh") * lax.axis_size("x") * lax.axis_size("c")
    array = jax.ShapeDtypeStruct
    place = jnp.stack([core, lax.axis_index("yl"), lax.axis_index(("yh", "x", "c")), lax.axis_index("z")]).astype(i32)

    lanes = jnp.arange(width) // rows == lax.axis_index("z")
    spots = jnp.where(lanes, jnp.pad(jnp.tile(membership, ring), (0, width - ring * rows)), 0)
    tail = jnp.pad(jnp.stack([spots // DIGIT, spots % DIGIT]), ((0, PACK - 2), (0, 0))).astype(bf16)
    block = jnp.concatenate([points, tail])
    spread = lax.all_to_all(jnp.broadcast_to(block[None], (ring,) + block.shape), "z", 0, 0)

    landmarks = landmark_pool[landmark_ids]

    def load(which):
        return jnp.concatenate(
            [lax.dynamic_slice_in_dim(m, which * quarter, quarter, 0) for m in (landmarks, whitening)]
        )

    up = hop(load(2 * core), ("yh", "yl"), 1)
    down = hop(load(2 * core + 1), ("yh", "yl"), -1)
    up_o, down_o = flip(up, "c", 1), flip(down, "c", 1)
    anchors, maps, factor = call(
        prepare_kernel,
        (array((2 * count, width), bf16), array((2 * count, rank_width), bf16), array((8, 2 * count), f32)),
        7,
        nbytes=8 * MIB,
    )(place, landmarks, whitening, up, down, up_o, down_o)

    kernel, keep, send = call(
        functools.partial(affinity_kernel, rows),
        (
            array((ring * rows, 2 * count), bf16),
            array((half, 2 * count + TALLY), bf16),
            array((half, 2 * count + TALLY), bf16),
        ),
        4,
        [pltpu.VMEM((clusters, ring * rows), bf16)],
        flops=2 * ring * rows * 2 * count * (width + clusters),
        nbytes=6 * MIB,
    )(place, spread, anchors, factor)

    theirs = flip(send, "c", 1)
    paired = (keep.astype(f32) + theirs.astype(f32)).astype(bf16)
    gathered = lax.all_to_all(paired.reshape(peers, share, -1), PLANE, 0, 0)

    near = ring // 2 - 1

    def project(first, dtypes, after=()):
        return call(
            functools.partial(project_kernel, first),
            tuple(array((rows, rank_width), dtype) for dtype in dtypes),
            3 + len(after),
            flops=2 * len(dtypes) * rows * 2 * count * rank_width,
            nbytes=3 * MIB,
        )(place, kernel, maps, *after)

    far = project(near, [bf16] * (ring - 2 * near + 1))
    parts = [hop(part, ("z",), near + i) for i, part in enumerate(far)]

    mapped, number = call(
        cluster_kernel,
        (array((share, rank_width), f32), array((share, rank_width), f32)),
        3 + len(parts),
        nbytes=3 * MIB,
    )(place, gathered, maps, *parts)
    bit = 1
    while bit < ring:
        mapped = mapped + flip(mapped, "z", bit)
        bit *= 2
    means = (mapped / number).astype(bf16)

    ahead = project(0, [f32] + [bf16] * (near - 1), (means,))
    behind = project(ring - near + 1, [bf16] * (near - 1), (means,))
    parts += [hop(part, ("z",), 1 + i) for i, part in enumerate(ahead[1:])]
    parts += [hop(part, ("z",), ring - near + 1 + i) for i, part in enumerate(behind)]
    sent = jnp.broadcast_to(means[None], (peers, share, rank_width))
    mine = lax.all_to_all(sent, PLANE, 0, 0).reshape(half, rank_width)
    features, choose, mine = call(
        feature_kernel,
        (
            array((rows, rank_width), bf16),
            array((clusters // groups, clusters), bf16),
            array((half, rank_width), bf16),
        ),
        3 + ring,
        nbytes=2 * MIB,
    )(place, owner_map.reshape(1, clusters), mine, ahead[0], *parts)
    other = flip(mine, "c", 1)
    near_scores, near_owned = call(
        near_kernel, (array((rows, half), f32), array((clusters // groups, rank_width), f32)), 4, nbytes=MIB
    )(place, features, mine, choose)
    scores, owned = call(
        far_kernel, (array((rows, clusters), f32), array((clusters // groups, rank_width), bf16)), 6, nbytes=MIB
    )(place, features, other, choose, near_scores, near_owned)
    return (features, owned, scores)


def build(mesh, factors):
    fine = Mesh(mesh.devices.reshape(factors), ALL)
    blk, dp = ("z", "yl"), ("yh", "x", "c")
    return jax.shard_map(
        body,
        mesh=fine,
        in_specs=(P(ALL, None), P(ALL), P(blk, None), P(blk), P(blk, None), P()),
        out_specs=(P(ALL, None), P(dp, None), P(ALL, None)),
        check_vma=False,
    )


def solution(mesh):
    return build(mesh, (4, 4, 2, 8, 2))
```

```python
import functools
import math

import jax
import jax.numpy as jnp
from jax import lax
from jax.experimental import pallas as pl
from jax.experimental.pallas import tpu as pltpu
from jax.sharding import Mesh, PartitionSpec as P

epsilon = 1e-06
bf16 = jnp.bfloat16
f32 = jnp.float32
i32 = jnp.int32
ALL = ("yh", "x", "c", "z", "yl")
PLANE = ("yh", "x", "yl")
PACK = 16
DIGIT = 128
TALLY = 128
MIB = 1 << 20


def hop(value, axis, by):
    size = math.prod(lax.axis_size(name) for name in axis)
    return lax.ppermute(value, axis, [(i, (i + by) % size) for i in range(size)])


def flip(value, axis, bit):
    size = lax.axis_size(axis)
    return lax.ppermute(value, axis, [(i, i ^ bit) for i in range(size)])


def across(a, b):
    return lax.dot_general(a, b, (((1,), (1,)), ((), ())), preferred_element_type=f32)


def call(kernel, out, ins, held=0, scratch=(), flops=0, nbytes=0):
    spec = pl.BlockSpec(memory_space=pltpu.VMEM)
    away = pl.BlockSpec(memory_space=pl.ANY)
    return pl.pallas_call(
        kernel,
        out_shape=out,
        in_specs=[pl.BlockSpec(memory_space=pltpu.SMEM)] + [spec] * (ins - 1 - held) + [away] * held,
        out_specs=jax.tree.map(lambda _: spec, out),
        scratch_shapes=list(scratch),
        compiler_params=pltpu.CompilerParams(vmem_limit_bytes=16 * MIB),
        cost_estimate=pl.CostEstimate(flops=flops, bytes_accessed=nbytes, transcendentals=0),
    )


def fetch(place, block, swapped, second, table, sems):
    core, half = place[0], place[1]
    count = block.shape[0]
    quarter = count // 4
    copies = [pltpu.make_async_copy(block, table.at[pl.ds(pl.multiple_of(half * count, count), count), :], sems.at[0])]
    for i, piece in enumerate(swapped):
        which = core if i < 2 else 1 - core
        at = pl.multiple_of((1 - half) * count + (2 * which + i % 2) * quarter, quarter)
        source = piece.at[pl.ds(second * quarter, quarter), :]
        copies.append(pltpu.make_async_copy(source, table.at[pl.ds(at, quarter), :], sems.at[1 + i]))
    for copy in copies:
        copy.start()
    return copies


def store(count, width):
    return [pltpu.VMEM((count, width), bf16), pltpu.SemaphoreType.DMA((5,))]


def row_squares(matrix):
    square = jnp.square(matrix.astype(f32))
    high = square.astype(bf16)
    low = (square - high.astype(f32)).astype(bf16)
    ones = jnp.ones((8, matrix.shape[1]), bf16)
    return across(ones, high) + across(ones, low)


def affinity_kernel(rows, place, spread, own, up, down, up_o, down_o, kernel, keep, send, table, anchors, sems):
    copies = fetch(place, own, (up, down, up_o, down_o), 0, anchors, sems)
    core = place[0]
    ring, _, width = spread.shape
    half = keep.shape[0]
    count = anchors.shape[0]
    points = ring * rows
    codes = jnp.sum(spread[:, rows:, :].astype(f32), axis=0)
    members = (codes[0:1, :points] * DIGIT + codes[1:2, :points]).astype(i32)
    label = lax.broadcasted_iota(i32, (half, points), 0)
    for ref, part in ((keep, 0), (send, 1)):
        which = jnp.where(core == 0, part, 1 - part)
        hit = jnp.where(label + which * half == members, 1.0, 0.0)
        table[part * half : (part + 1) * half, :] = hit.astype(bf16)
        tally = jnp.sum(hit, axis=1, keepdims=True)
        big = jnp.floor(tally * (1.0 / DIGIT))
        lane = lax.broadcasted_iota(i32, (half, TALLY), 1)
        digits = jnp.where(lane == 0, big, jnp.where(lane == 1, tally - big * DIGIT, 0.0))
        ref[:, count:] = digits.astype(bf16)
    visitors = spread[:, :rows, :].reshape(points, width)
    length = lax.rsqrt(jnp.sum(jnp.square(visitors.astype(f32)), axis=1, keepdims=True) + epsilon) * math.sqrt(width)
    for copy in copies:
        copy.wait()
    tile = min(256, count)

    @pl.loop(0, count // tile)
    def _(j):
        at = pl.multiple_of(j * tile, tile)
        values = spread[:, :rows, :].reshape(points, width)
        marks = anchors[pl.ds(at, tile), :]
        factor = lax.rsqrt(row_squares(marks) + epsilon)[0:1]
        part = jnp.exp(across(values, marks) * length * factor).astype(bf16)
        kernel[:, pl.ds(at, tile)] = part
        sums = jnp.dot(table[...], part, preferred_element_type=f32).astype(bf16)
        keep[:, pl.ds(at, tile)] = sums[:half]
        send[:, pl.ds(at, tile)] = sums[half:]


def project(place, kernel, maps, owners, rows, at, tile):
    spots = [pl.multiple_of(lax.bitwise_xor(place[3], d) * rows, rows) for d in owners]
    span = jnp.concatenate([kernel[pl.ds(spot, rows), :] for spot in spots])
    return jnp.dot(span, maps[:, pl.ds(at, tile)], preferred_element_type=f32)


def away_kernel(owners, place, kernel, white, up, down, up_o, down_o, send, maps, sems):
    copies = fetch(place, white, (up, down, up_o, down_o), 1, maps, sems)
    for copy in copies:
        copy.wait()
    rows, width = send.shape[0] // len(owners), send.shape[1]
    tile = min(256, width)

    @pl.loop(0, width // tile)
    def _(j):
        at = pl.multiple_of(j * tile, tile)
        send[:, pl.ds(at, tile)] = project(place, kernel, maps, owners, rows, at, tile).astype(bf16)


def stay_kernel(owners, place, kernel, arrived, white, up, down, up_o, down_o, keep, send, maps, sems):
    copies = fetch(place, white, (up, down, up_o, down_o), 1, maps, sems)
    for copy in copies:
        copy.wait()
    rows, width = arrived.shape[0] // len(owners), arrived.shape[1]
    tile = min(256, width)
    half = keep.shape[0]

    @pl.loop(0, width // tile)
    def _(j):
        at = pl.multiple_of(j * tile, tile)
        both = project(place, kernel, maps, owners, rows, at, tile) + arrived[:, pl.ds(at, tile)].astype(f32)
        keep[:, pl.ds(at, tile)] = both[:half]
        send[:, pl.ds(at, tile)] = both[half:].astype(bf16)


def cluster_kernel(place, spread, *rest):
    white, up, down, up_o, down_o = rest[-9:-4]
    mapped, number, maps, sems = rest[-4:]
    copies = fetch(place, white, (up, down, up_o, down_o), 1, maps, sems)
    count = maps.shape[0]
    share = spread.shape[1]
    total = jnp.sum(spread[...].astype(f32), axis=0)
    sums = total[:, :count]
    high = sums.astype(bf16).astype(f32)
    both = jnp.concatenate([high, sums - high]).astype(bf16)
    tally = total[:, count : count + 1] * DIGIT + total[:, count + 1 : count + 2]
    number[...] = jnp.broadcast_to(jnp.maximum(tally, 1.0), number.shape)
    for copy in copies:
        copy.wait()
    result = jnp.dot(both, maps[...], preferred_element_type=f32)
    mapped[...] = result[:share] + result[share:]


def merge_kernel(place, kept, arrived, _, keep, send):
    rows = keep.shape[0]
    both = kept[...] + arrived[...].astype(f32)
    keep[...] = both[:rows]
    send[...] = both[rows:].astype(bf16)


def feature_kernel(place, owners, *rest):
    arrived, kept, last, features, choose, means = rest
    means[...] = arrived[...]
    features[...] = (kept[...] + last[...].astype(f32)).astype(bf16)
    slots, clusters = choose.shape
    owned = owners[...] == place[2]
    row = lax.broadcasted_iota(i32, (clusters, clusters), 0)
    col = lax.broadcasted_iota(i32, (clusters, clusters), 1)
    before = jnp.where(row < col, 1.0, 0.0).astype(bf16)
    mark = jnp.broadcast_to(jnp.where(owned, 1.0, 0.0), (slots, clusters))
    rank = jnp.dot(mark.astype(bf16), before, preferred_element_type=f32)
    slot = lax.broadcasted_iota(i32, (slots, clusters), 0).astype(f32)
    choose[...] = jnp.where(rank == slot, mark, 0.0).astype(bf16)


def half_scores(features, means, choose, at):
    half = means.shape[0]
    norms = row_squares(means[...])[0:1]
    scores = (norms - 2.0 * across(features[...], means[...])) * (1.0 / means.shape[1])
    owned = jnp.dot(choose[:, pl.ds(at, half)], means[...], preferred_element_type=f32)
    return scores, owned


def near_kernel(place, features, means, choose, scores, owned):
    half = means.shape[0]
    at = pl.multiple_of(place[0] * half, half)
    scores[...], owned[...] = half_scores(features, means, choose, at)


def far_kernel(place, features, means, choose, near_scores, near_owned, scores, owned):
    half = means.shape[0]
    there = pl.multiple_of((1 - place[0]) * half, half)
    here = pl.multiple_of(place[0] * half, half)
    far, rest = half_scores(features, means, choose, there)
    scores[:, pl.ds(there, half)] = far
    scores[:, pl.ds(here, half)] = near_scores[...]
    owned[...] = (near_owned[...] + rest).astype(bf16)


def body(points, membership, landmark_pool, landmark_ids, whitening, owner_map):
    rows, width = points.shape
    count, rank_width = whitening.shape
    clusters = owner_map.shape[0]
    ring = lax.axis_size("z")
    core = lax.axis_index("c")
    quarter = count // 4
    half = clusters // 2
    peers = math.prod(lax.axis_size(name) for name in PLANE)
    share = half // peers
    groups = lax.axis_size("yh") * lax.axis_size("x") * lax.axis_size("c")
    array = jax.ShapeDtypeStruct
    place = jnp.stack([core, lax.axis_index("yl"), lax.axis_index(("yh", "x", "c")), lax.axis_index("z")]).astype(i32)

    lanes = jnp.arange(width) // rows == lax.axis_index("z")
    spots = jnp.where(lanes, jnp.pad(jnp.tile(membership, ring), (0, width - ring * rows)), 0)
    tail = jnp.pad(jnp.stack([spots // DIGIT, spots % DIGIT]), ((0, PACK - 2), (0, 0))).astype(bf16)
    block = jnp.concatenate([points, tail])
    spread = lax.all_to_all(jnp.broadcast_to(block[None], (ring,) + block.shape), "z", 0, 0)

    landmarks = landmark_pool[landmark_ids]

    def load(which):
        return jnp.concatenate(
            [lax.dynamic_slice_in_dim(m, which * quarter, quarter, 0) for m in (landmarks, whitening)]
        )

    up = hop(load(2 * core), ("yh", "yl"), 1)
    down = hop(load(2 * core + 1), ("yh", "yl"), -1)
    up_o, down_o = flip(up, "c", 1), flip(down, "c", 1)
    pieces = (up, down, up_o, down_o)

    kernel, keep, send = call(
        functools.partial(affinity_kernel, rows),
        (
            array((ring * rows, 2 * count), bf16),
            array((half, 2 * count + TALLY), bf16),
            array((half, 2 * count + TALLY), bf16),
        ),
        7,
        5,
        [pltpu.VMEM((clusters, ring * rows), bf16)] + store(2 * count, width),
        flops=2 * ring * rows * 2 * count * (width + clusters),
        nbytes=6 * MIB,
    )(place, spread, landmarks, *pieces)

    theirs = flip(send, "c", 1)
    paired = (keep.astype(f32) + theirs.astype(f32)).astype(bf16)
    gathered = lax.all_to_all(paired.reshape(peers, share, -1), PLANE, 0, 0)

    leave = call(
        functools.partial(away_kernel, (1, 6, 2, 5)),
        array((ring // 2 * rows, rank_width), bf16),
        7,
        5,
        store(2 * count, rank_width),
        flops=ring * rows * 2 * count * rank_width,
        nbytes=3 * MIB,
    )(place, kernel, whitening, *pieces)
    arrived = flip(leave, "z", 1)
    kept, leave = call(
        functools.partial(stay_kernel, (0, 7, 3, 4)),
        (array((ring // 4 * rows, rank_width), f32), array((ring // 4 * rows, rank_width), bf16)),
        8,
        5,
        store(2 * count, rank_width),
        flops=ring * rows * 2 * count * rank_width,
        nbytes=3 * MIB,
    )(place, kernel, arrived, whitening, *pieces)

    mapped, number = call(
        cluster_kernel,
        (array((share, rank_width), f32), array((share, rank_width), f32)),
        8,
        6,
        store(2 * count, rank_width),
        nbytes=3 * MIB,
    )(place, gathered, leave, whitening, *pieces)
    bit = 1
    while bit < ring:
        mapped = mapped + flip(mapped, "z", bit)
        bit *= 2
    means = (mapped / number).astype(bf16)

    sent = jnp.broadcast_to(means[None], (peers, share, rank_width))
    mine = lax.all_to_all(sent, PLANE, 0, 0).reshape(half, rank_width)

    arrived = flip(leave, "z", 3)
    kept, leave = call(
        merge_kernel,
        (array((rows, rank_width), f32), array((rows, rank_width), bf16)),
        4,
        1,
        nbytes=MIB,
    )(place, kept, arrived, means)
    last = flip(leave, "z", 7)
    features, choose, mine = call(
        feature_kernel,
        (
            array((rows, rank_width), bf16),
            array((clusters // groups, clusters), bf16),
            array((half, rank_width), bf16),
        ),
        5,
        nbytes=2 * MIB,
    )(place, owner_map.reshape(1, clusters), mine, kept, last)
    other = flip(mine, "c", 1)
    near_scores, near_owned = call(
        near_kernel, (array((rows, half), f32), array((clusters // groups, rank_width), f32)), 4, nbytes=MIB
    )(place, features, mine, choose)
    scores, owned = call(
        far_kernel, (array((rows, clusters), f32), array((clusters // groups, rank_width), bf16)), 6, nbytes=MIB
    )(place, features, other, choose, near_scores, near_owned)
    return (features, owned, scores)


def build(mesh, factors):
    fine = Mesh(mesh.devices.reshape(factors), ALL)
    blk, dp = ("z", "yl"), ("yh", "x", "c")
    return jax.shard_map(
        body,
        mesh=fine,
        in_specs=(P(ALL, None), P(ALL), P(blk, None), P(blk), P(blk, None), P()),
        out_specs=(P(ALL, None), P(dp, None), P(ALL, None)),
        check_vma=False,
    )


def solution(mesh):
    return build(mesh, (4, 4, 2, 8, 2))
```

```python
import functools
import math

import jax
import jax.numpy as jnp
from jax import lax
from jax.experimental import pallas as pl
from jax.experimental.pallas import tpu as pltpu
from jax.sharding import Mesh, PartitionSpec as P

epsilon = 1e-06
bf16 = jnp.bfloat16
f32 = jnp.float32
i32 = jnp.int32
ALL = ("yh", "x", "c", "z", "yl")
PLANE = ("yh", "x", "yl")
PACK = 16
DIGIT = 128
TALLY = 128
MIB = 1 << 20


def hop(value, axis, by):
    size = math.prod(lax.axis_size(name) for name in axis)
    return lax.ppermute(value, axis, [(i, (i + by) % size) for i in range(size)])


def flip(value, axis, bit):
    size = lax.axis_size(axis)
    return lax.ppermute(value, axis, [(i, i ^ bit) for i in range(size)])


def across(a, b):
    return lax.dot_general(a, b, (((1,), (1,)), ((), ())), preferred_element_type=f32)


def call(kernel, out, ins, held=0, scratch=(), flops=0, nbytes=0):
    spec = pl.BlockSpec(memory_space=pltpu.VMEM)
    away = pl.BlockSpec(memory_space=pl.ANY)
    return pl.pallas_call(
        kernel,
        out_shape=out,
        in_specs=[pl.BlockSpec(memory_space=pltpu.SMEM)] + [spec] * (ins - 1 - held) + [away] * held,
        out_specs=jax.tree.map(lambda _: spec, out),
        scratch_shapes=list(scratch),
        compiler_params=pltpu.CompilerParams(vmem_limit_bytes=16 * MIB),
        cost_estimate=pl.CostEstimate(flops=flops, bytes_accessed=nbytes, transcendentals=0),
    )


def fetch(place, block, swapped, second, table, sems):
    core, half = place[0], place[1]
    count = block.shape[0]
    quarter = count // 4
    copies = [pltpu.make_async_copy(block, table.at[pl.ds(pl.multiple_of(half * count, count), count), :], sems.at[0])]
    for i, piece in enumerate(swapped):
        which = core if i < 2 else 1 - core
        at = pl.multiple_of((1 - half) * count + (2 * which + i % 2) * quarter, quarter)
        source = piece.at[pl.ds(second * quarter, quarter), :]
        copies.append(pltpu.make_async_copy(source, table.at[pl.ds(at, quarter), :], sems.at[1 + i]))
    for copy in copies:
        copy.start()
    return copies


def store(count, width):
    return [pltpu.VMEM((count, width), bf16), pltpu.SemaphoreType.DMA((5,))]


def row_squares(matrix):
    square = jnp.square(matrix.astype(f32))
    high = square.astype(bf16)
    low = (square - high.astype(f32)).astype(bf16)
    ones = jnp.ones((8, matrix.shape[1]), bf16)
    return across(ones, high) + across(ones, low)


def affinity_kernel(rows, place, spread, own, up, down, up_o, down_o, kernel, keep, send, table, anchors, sems):
    copies = fetch(place, own, (up, down, up_o, down_o), 0, anchors, sems)
    core = place[0]
    ring, _, width = spread.shape
    half = keep.shape[0]
    count = anchors.shape[0]
    points = ring * rows
    codes = jnp.sum(spread[:, rows:, :].astype(f32), axis=0)
    members = (codes[0:1, :points] * DIGIT + codes[1:2, :points]).astype(i32)
    label = lax.broadcasted_iota(i32, (half, points), 0)
    for ref, part in ((keep, 0), (send, 1)):
        which = jnp.where(core == 0, part, 1 - part)
        hit = jnp.where(label + which * half == members, 1.0, 0.0)
        table[part * half : (part + 1) * half, :] = hit.astype(bf16)
        tally = jnp.sum(hit, axis=1, keepdims=True)
        big = jnp.floor(tally * (1.0 / DIGIT))
        lane = lax.broadcasted_iota(i32, (half, TALLY), 1)
        digits = jnp.where(lane == 0, big, jnp.where(lane == 1, tally - big * DIGIT, 0.0))
        ref[:, count:] = digits.astype(bf16)
    visitors = spread[:, :rows, :].reshape(points, width)
    length = lax.rsqrt(jnp.sum(jnp.square(visitors.astype(f32)), axis=1, keepdims=True) + epsilon) * math.sqrt(width)
    for copy in copies:
        copy.wait()
    tile = min(256, count)

    for at in range(0, count, tile):
        values = spread[:, :rows, :].reshape(points, width)
        marks = anchors[pl.ds(at, tile), :]
        factor = lax.rsqrt(row_squares(marks) + epsilon)[0:1]
        part = jnp.exp(across(values, marks) * length * factor).astype(bf16)
        kernel[:, pl.ds(at, tile)] = part
        sums = jnp.dot(table[...], part, preferred_element_type=f32).astype(bf16)
        keep[:, pl.ds(at, tile)] = sums[:half]
        send[:, pl.ds(at, tile)] = sums[half:]


def project(place, kernel, maps, owners, rows, at, tile):
    spots = [pl.multiple_of(lax.bitwise_xor(place[3], d) * rows, rows) for d in owners]
    span = jnp.concatenate([kernel[pl.ds(spot, rows), :] for spot in spots])
    return jnp.dot(span, maps[:, pl.ds(at, tile)], preferred_element_type=f32)


def away_kernel(owners, place, kernel, white, up, down, up_o, down_o, send, maps, sems):
    copies = fetch(place, white, (up, down, up_o, down_o), 1, maps, sems)
    for copy in copies:
        copy.wait()
    rows, width = send.shape[0] // len(owners), send.shape[1]
    tile = min(256, width)

    for at in range(0, width, tile):
        send[:, pl.ds(at, tile)] = project(place, kernel, maps, owners, rows, at, tile).astype(bf16)


def stay_kernel(owners, place, kernel, arrived, white, up, down, up_o, down_o, keep, send, maps, sems):
    copies = fetch(place, white, (up, down, up_o, down_o), 1, maps, sems)
    for copy in copies:
        copy.wait()
    rows, width = arrived.shape[0] // len(owners), arrived.shape[1]
    tile = min(256, width)
    half = keep.shape[0]

    for at in range(0, width, tile):
        both = project(place, kernel, maps, owners, rows, at, tile) + arrived[:, pl.ds(at, tile)].astype(f32)
        keep[:, pl.ds(at, tile)] = both[:half]
        send[:, pl.ds(at, tile)] = both[half:].astype(bf16)


def cluster_kernel(place, spread, *rest):
    white, up, down, up_o, down_o = rest[-9:-4]
    mapped, number, maps, sems = rest[-4:]
    copies = fetch(place, white, (up, down, up_o, down_o), 1, maps, sems)
    count = maps.shape[0]
    share = spread.shape[1]
    total = jnp.sum(spread[...].astype(f32), axis=0)
    sums = total[:, :count]
    high = sums.astype(bf16).astype(f32)
    both = jnp.concatenate([high, sums - high]).astype(bf16)
    tally = total[:, count : count + 1] * DIGIT + total[:, count + 1 : count + 2]
    number[...] = jnp.broadcast_to(jnp.maximum(tally, 1.0), number.shape)
    for copy in copies:
        copy.wait()
    result = jnp.dot(both, maps[...], preferred_element_type=f32)
    mapped[...] = jnp.broadcast_to((result[:share] + result[share:])[None], mapped.shape)


def merge_kernel(place, kept, arrived, _, keep, send):
    rows = keep.shape[0]
    both = kept[...] + arrived[...].astype(f32)
    keep[...] = both[:rows]
    send[...] = both[rows:].astype(bf16)


def pair_kernel(place, keep, theirs, _, paired):
    paired[...] = (keep[...].astype(f32) + theirs[...].astype(f32)).astype(bf16)


def means_kernel(place, parts, number, _, sent):
    means = jnp.sum(parts[...], axis=0) / number[...]
    sent[...] = jnp.broadcast_to(means[None], sent.shape).astype(bf16)


def feature_kernel(place, owners, *rest):
    arrived, kept, last, features, choose, means = rest
    means[...] = arrived[...]
    features[...] = (kept[...] + last[...].astype(f32)).astype(bf16)
    slots, clusters = choose.shape
    owned = owners[...] == place[2]
    row = lax.broadcasted_iota(i32, (clusters, clusters), 0)
    col = lax.broadcasted_iota(i32, (clusters, clusters), 1)
    before = jnp.where(row < col, 1.0, 0.0).astype(bf16)
    mark = jnp.broadcast_to(jnp.where(owned, 1.0, 0.0), (slots, clusters))
    rank = jnp.dot(mark.astype(bf16), before, preferred_element_type=f32)
    slot = lax.broadcasted_iota(i32, (slots, clusters), 0).astype(f32)
    choose[...] = jnp.where(rank == slot, mark, 0.0).astype(bf16)


def half_scores(features, means, choose, at):
    half = means.shape[0]
    norms = row_squares(means[...])[0:1]
    scores = (norms - 2.0 * across(features[...], means[...])) * (1.0 / means.shape[1])
    owned = jnp.dot(choose[:, pl.ds(at, half)], means[...], preferred_element_type=f32)
    return scores, owned


def near_kernel(place, features, means, choose, scores, owned):
    half = means.shape[0]
    at = pl.multiple_of(place[0] * half, half)
    scores[...], owned[...] = half_scores(features, means, choose, at)


def far_kernel(place, features, means, choose, near_scores, near_owned, scores, owned):
    half = means.shape[0]
    there = pl.multiple_of((1 - place[0]) * half, half)
    here = pl.multiple_of(place[0] * half, half)
    far, rest = half_scores(features, means, choose, there)
    scores[:, pl.ds(there, half)] = far
    scores[:, pl.ds(here, half)] = near_scores[...]
    owned[...] = (near_owned[...] + rest).astype(bf16)


def body(points, membership, landmark_pool, landmark_ids, whitening, owner_map):
    rows, width = points.shape
    count, rank_width = whitening.shape
    clusters = owner_map.shape[0]
    ring = lax.axis_size("z")
    core = lax.axis_index("c")
    quarter = count // 4
    half = clusters // 2
    peers = math.prod(lax.axis_size(name) for name in PLANE)
    share = half // peers
    groups = lax.axis_size("yh") * lax.axis_size("x") * lax.axis_size("c")
    array = jax.ShapeDtypeStruct
    place = jnp.stack([core, lax.axis_index("yl"), lax.axis_index(("yh", "x", "c")), lax.axis_index("z")]).astype(i32)

    lanes = jnp.arange(width) // rows == lax.axis_index("z")
    spots = jnp.where(lanes, jnp.pad(jnp.tile(membership, ring), (0, width - ring * rows)), 0)
    tail = jnp.pad(jnp.stack([spots // DIGIT, spots % DIGIT]), ((0, PACK - 2), (0, 0))).astype(bf16)
    block = jnp.concatenate([points, tail])
    spread = lax.all_to_all(jnp.broadcast_to(block[None], (ring,) + block.shape), "z", 0, 0)

    landmarks = landmark_pool[landmark_ids]

    def load(which):
        return jnp.concatenate(
            [lax.dynamic_slice_in_dim(m, which * quarter, quarter, 0) for m in (landmarks, whitening)]
        )

    up = hop(load(2 * core), ("yh", "yl"), 1)
    down = hop(load(2 * core + 1), ("yh", "yl"), -1)
    up_o, down_o = flip(up, "c", 1), flip(down, "c", 1)
    pieces = (up, down, up_o, down_o)

    kernel, keep, send = call(
        functools.partial(affinity_kernel, rows),
        (
            array((ring * rows, 2 * count), bf16),
            array((half, 2 * count + TALLY), bf16),
            array((half, 2 * count + TALLY), bf16),
        ),
        7,
        5,
        [pltpu.VMEM((clusters, ring * rows), bf16)] + store(2 * count, width),
        flops=2 * ring * rows * 2 * count * (width + clusters),
        nbytes=6 * MIB,
    )(place, spread, landmarks, *pieces)

    theirs = flip(send, "c", 1)
    leave = call(
        functools.partial(away_kernel, (1, 6, 2, 5)),
        array((ring // 2 * rows, rank_width), bf16),
        7,
        5,
        store(2 * count, rank_width),
        flops=ring * rows * 2 * count * rank_width,
        nbytes=3 * MIB,
    )(place, kernel, whitening, *pieces)
    paired = call(pair_kernel, array(keep.shape, bf16), 4, 1, nbytes=2 * MIB)(place, keep, theirs, leave)
    gathered = lax.all_to_all(paired.reshape(peers, share, -1), PLANE, 0, 0)
    arrived = flip(leave, "z", 1)
    kept, leave = call(
        functools.partial(stay_kernel, (0, 7, 3, 4)),
        (array((ring // 4 * rows, rank_width), f32), array((ring // 4 * rows, rank_width), bf16)),
        8,
        5,
        store(2 * count, rank_width),
        flops=ring * rows * 2 * count * rank_width,
        nbytes=3 * MIB,
    )(place, kernel, arrived, whitening, *pieces)

    mapped, number = call(
        cluster_kernel,
        (array((ring, share, rank_width), f32), array((share, rank_width), f32)),
        8,
        6,
        store(2 * count, rank_width),
        nbytes=3 * MIB,
    )(place, gathered, arrived, whitening, *pieces)
    over = lax.all_to_all(mapped, "z", 0, 0)
    sent = call(means_kernel, array((peers, share, rank_width), bf16), 4, 1, nbytes=MIB)(place, over, number, leave)
    mine = lax.all_to_all(sent, PLANE, 0, 0).reshape(half, rank_width)

    arrived = flip(leave, "z", 3)
    kept, leave = call(
        merge_kernel,
        (array((rows, rank_width), f32), array((rows, rank_width), bf16)),
        4,
        1,
        nbytes=MIB,
    )(place, kept, arrived, sent)
    last = flip(leave, "z", 7)
    features, choose, mine = call(
        feature_kernel,
        (
            array((rows, rank_width), bf16),
            array((clusters // groups, clusters), bf16),
            array((half, rank_width), bf16),
        ),
        5,
        nbytes=2 * MIB,
    )(place, owner_map.reshape(1, clusters), mine, kept, last)
    other = flip(mine, "c", 1)
    near_scores, near_owned = call(
        near_kernel, (array((rows, half), f32), array((clusters // groups, rank_width), f32)), 4, nbytes=MIB
    )(place, features, mine, choose)
    scores, owned = call(
        far_kernel, (array((rows, clusters), f32), array((clusters // groups, rank_width), bf16)), 6, nbytes=MIB
    )(place, features, other, choose, near_scores, near_owned)
    return (features, owned, scores)


def build(mesh, factors):
    fine = Mesh(mesh.devices.reshape(factors), ALL)
    blk, dp = ("z", "yl"), ("yh", "x", "c")
    return jax.shard_map(
        body,
        mesh=fine,
        in_specs=(P(ALL, None), P(ALL), P(blk, None), P(blk), P(blk, None), P()),
        out_specs=(P(ALL, None), P(dp, None), P(ALL, None)),
        check_vma=False,
    )


def solution(mesh):
    return build(mesh, (4, 4, 2, 8, 2))
```

```python
import functools
import math

import jax
import jax.numpy as jnp
from jax import lax
from jax.experimental import pallas as pl
from jax.experimental.pallas import tpu as pltpu
from jax.sharding import Mesh, PartitionSpec as P

epsilon = 1e-06
bf16 = jnp.bfloat16
f32 = jnp.float32
i32 = jnp.int32
ALL = ("yh", "x", "c", "z", "yl")
PLANE = ("yh", "x", "yl")
PACK = 16
LEAVE = (1, 6, 2, 5)
STAY = (0, 7, 3, 4)
DIGIT = 128
TALLY = 128
MIB = 1 << 20


def hop(value, axis, by):
    size = math.prod(lax.axis_size(name) for name in axis)
    return lax.ppermute(value, axis, [(i, (i + by) % size) for i in range(size)])


def flip(value, axis, bit):
    size = lax.axis_size(axis)
    return lax.ppermute(value, axis, [(i, i ^ bit) for i in range(size)])


def across(a, b):
    return lax.dot_general(a, b, (((1,), (1,)), ((), ())), preferred_element_type=f32)


def call(kernel, out, ins, held=0, scratch=(), away=(), flops=0, nbytes=0):
    spec = pl.BlockSpec(memory_space=pltpu.VMEM)
    far = pl.BlockSpec(memory_space=pltpu.HBM)
    scratch, many = list(scratch), len(out)
    own = len(scratch)
    for i in away:
        scratch += [pltpu.VMEM(out[i].shape, out[i].dtype), pltpu.SemaphoreType.DMA]

    def run(*refs):
        outs, extra = list(refs[ins : ins + many]), refs[ins + many :]
        moves = []
        for n, i in enumerate(away):
            staged, sem = extra[own + 2 * n : own + 2 * n + 2]
            moves.append(pltpu.make_async_copy(staged, outs[i], sem))
            outs[i] = staged
        kernel(*refs[:ins], *outs, *extra[:own])
        for move in moves:
            move.start()
        for move in moves:
            move.wait()

    made = pl.pallas_call(
        run,
        out_shape=tuple(pltpu.HBM(o.shape, o.dtype) if i in away else o for i, o in enumerate(out)),
        in_specs=[pl.BlockSpec(memory_space=pltpu.SMEM)] + [spec] * (ins - 1 - held) + [far] * held,
        out_specs=tuple(far if i in away else spec for i in range(many)),
        scratch_shapes=scratch,
        compiler_params=pltpu.CompilerParams(vmem_limit_bytes=16 * MIB),
        cost_estimate=pl.CostEstimate(flops=flops, bytes_accessed=nbytes, transcendentals=0),
    )
    near = ins - held
    return lambda *args: made(*args[:near], *(pltpu.with_memory_space_constraint(a, pltpu.HBM) for a in args[near:]))


def fetch(place, block, swapped, second, table, sems):
    core, half = place[0], place[1]
    count = block.shape[0]
    quarter = count // 4
    copies = [pltpu.make_async_copy(block, table.at[pl.ds(pl.multiple_of(half * count, count), count), :], sems.at[0])]
    for i, piece in enumerate(swapped):
        which = core if i < 2 else 1 - core
        at = pl.multiple_of((1 - half) * count + (2 * which + i % 2) * quarter, quarter)
        source = piece.at[pl.ds(second * quarter, quarter), :]
        copies.append(pltpu.make_async_copy(source, table.at[pl.ds(at, quarter), :], sems.at[1 + i]))
    for copy in copies:
        copy.start()
    return copies


def store(count, width):
    return [pltpu.VMEM((count, width), bf16), pltpu.SemaphoreType.DMA((5,))]


def row_squares(matrix):
    square = jnp.square(matrix.astype(f32))
    high = square.astype(bf16)
    low = (square - high.astype(f32)).astype(bf16)
    ones = jnp.ones((8, matrix.shape[1]), bf16)
    return across(ones, high) + across(ones, low)


def pack_kernel(place, points, members, out):
    rows, width = points.shape
    code = jnp.broadcast_to(members[...], (PACK, rows))
    row = lax.broadcasted_iota(i32, (PACK, rows), 0)
    digits = jnp.where(row == 0, code // DIGIT, jnp.where(row == 1, code % DIGIT, 0)).astype(f32).astype(bf16)
    lane = lax.broadcasted_iota(i32, (rows, width), 1) - place[3] * rows
    spot = jnp.where(lane == lax.broadcasted_iota(i32, (rows, width), 0), 1.0, 0.0).astype(bf16)
    tail = jnp.dot(digits, spot, preferred_element_type=f32).astype(bf16)
    for i in range(out.shape[0]):
        out[i, :rows, :] = points[...]
        out[i, rows:, :] = tail


def affinity_kernel(rows, place, spread, own, up, down, up_o, down_o, kernel, keep, send, table, anchors, sems):
    copies = fetch(place, own, (up, down, up_o, down_o), 0, anchors, sems)
    core = place[0]
    ring, _, width = spread.shape
    half = keep.shape[0]
    count = anchors.shape[0]
    points = ring * rows
    codes = jnp.sum(spread[:, rows:, :].astype(f32), axis=0)
    members = (codes[0:1, :points] * DIGIT + codes[1:2, :points]).astype(i32)
    label = lax.broadcasted_iota(i32, (half, points), 0)
    for ref, part in ((keep, 0), (send, 1)):
        which = jnp.where(core == 0, part, 1 - part)
        hit = jnp.where(label + which * half == members, 1.0, 0.0)
        table[part * half : (part + 1) * half, :] = hit.astype(bf16)
        tally = jnp.sum(hit, axis=1, keepdims=True)
        big = jnp.floor(tally * (1.0 / DIGIT))
        lane = lax.broadcasted_iota(i32, (half, TALLY), 1)
        digits = jnp.where(lane == 0, big, jnp.where(lane == 1, tally - big * DIGIT, 0.0))
        ref[:, count:] = digits.astype(bf16)
    visitors = spread[:, :rows, :].reshape(points, width)
    length = lax.rsqrt(jnp.sum(jnp.square(visitors.astype(f32)), axis=1, keepdims=True) + epsilon) * math.sqrt(width)
    for copy in copies:
        copy.wait()
    tile = min(256, count)

    for at in range(0, count, tile):
        values = spread[:, :rows, :].reshape(points, width)
        marks = anchors[pl.ds(at, tile), :]
        factor = lax.rsqrt(row_squares(marks) + epsilon)[0:1]
        part = jnp.exp(across(values, marks) * length * factor).astype(bf16)
        kernel[:, pl.ds(at, tile)] = part
        sums = jnp.dot(table[...], part, preferred_element_type=f32).astype(bf16)
        keep[:, pl.ds(at, tile)] = sums[:half]
        send[:, pl.ds(at, tile)] = sums[half:]


def project(place, kernel, maps, owners, rows, at, tile):
    spots = [pl.multiple_of(lax.bitwise_xor(place[3], d) * rows, rows) for d in owners]
    span = jnp.concatenate([kernel[pl.ds(spot, rows), :] for spot in spots])
    return jnp.dot(span, maps[:, pl.ds(at, tile)], preferred_element_type=f32)


def project_kernel(kernel_rows, place, kernel, white, up, down, up_o, down_o, leave, stay, token, maps, sems):
    copies = fetch(place, white, (up, down, up_o, down_o), 1, maps, sems)
    for copy in copies:
        copy.wait()
    token[...] = jnp.zeros_like(token)
    width = leave.shape[1]
    tile = min(256, width)
    for at in range(0, width, tile):
        for out, owners in ((leave, LEAVE), (stay, STAY)):
            out[:, at : at + tile] = project(place, kernel, maps, owners, kernel_rows, at, tile).astype(bf16)


def merge_kernel(place, kept, arrived, keep, send, token):
    half = keep.shape[0]
    both = (kept[...].astype(f32) + arrived[...].astype(f32)).astype(bf16)
    keep[...] = both[:half]
    send[...] = both[half:]
    token[...] = jnp.zeros_like(token)


def cluster_kernel(place, spread, *rest):
    white, up, down, up_o, down_o = rest[-9:-4]
    mapped, number, maps, sems = rest[-4:]
    copies = fetch(place, white, (up, down, up_o, down_o), 1, maps, sems)
    count = maps.shape[0]
    share = spread.shape[1]
    total = jnp.sum(spread[...].astype(f32), axis=0)
    sums = total[:, :count]
    high = sums.astype(bf16).astype(f32)
    both = jnp.concatenate([high, sums - high]).astype(bf16)
    tally = total[:, count : count + 1] * DIGIT + total[:, count + 1 : count + 2]
    number[...] = jnp.broadcast_to(jnp.maximum(tally, 1.0), number.shape)
    for copy in copies:
        copy.wait()
    result = jnp.dot(both, maps[...], preferred_element_type=f32)
    mapped[...] = jnp.broadcast_to((result[:share] + result[share:])[None], mapped.shape)


def pair_kernel(place, keep, theirs, _, paired):
    paired[...] = (keep[...].astype(f32) + theirs[...].astype(f32)).astype(bf16)


def means_kernel(place, parts, number, _, sent):
    means = jnp.sum(parts[...], axis=0) / number[...]
    sent[...] = jnp.broadcast_to(means[None], sent.shape).astype(bf16)


def feature_kernel(place, owners, *rest):
    arrived, kept, last, features, choose, means = rest
    means[...] = arrived[...]
    features[...] = (kept[...].astype(f32) + last[...].astype(f32)).astype(bf16)
    slots, clusters = choose.shape
    owned = owners[...] == place[2]
    row = lax.broadcasted_iota(i32, (clusters, clusters), 0)
    col = lax.broadcasted_iota(i32, (clusters, clusters), 1)
    before = jnp.where(row < col, 1.0, 0.0).astype(bf16)
    mark = jnp.broadcast_to(jnp.where(owned, 1.0, 0.0), (slots, clusters))
    rank = jnp.dot(mark.astype(bf16), before, preferred_element_type=f32)
    slot = lax.broadcasted_iota(i32, (slots, clusters), 0).astype(f32)
    choose[...] = jnp.where(rank == slot, mark, 0.0).astype(bf16)


def half_scores(features, means, choose, at):
    half = means.shape[0]
    norms = row_squares(means[...])[0:1]
    scores = (norms - 2.0 * across(features[...], means[...])) * (1.0 / means.shape[1])
    owned = jnp.dot(choose[:, pl.ds(at, half)], means[...], preferred_element_type=f32)
    return scores, owned


def near_kernel(place, features, means, choose, scores, owned):
    half = means.shape[0]
    at = pl.multiple_of(place[0] * half, half)
    scores[...], owned[...] = half_scores(features, means, choose, at)


def far_kernel(place, features, means, choose, near_scores, near_owned, scores, owned):
    half = means.shape[0]
    there = pl.multiple_of((1 - place[0]) * half, half)
    here = pl.multiple_of(place[0] * half, half)
    far, rest = half_scores(features, means, choose, there)
    scores[:, pl.ds(there, half)] = far
    scores[:, pl.ds(here, half)] = near_scores[...]
    owned[...] = (near_owned[...] + rest).astype(bf16)


def body(points, membership, landmark_pool, landmark_ids, whitening, owner_map):
    rows, width = points.shape
    count, rank_width = whitening.shape
    clusters = owner_map.shape[0]
    ring = lax.axis_size("z")
    core = lax.axis_index("c")
    quarter = count // 4
    half = clusters // 2
    peers = math.prod(lax.axis_size(name) for name in PLANE)
    share = half // peers
    groups = lax.axis_size("yh") * lax.axis_size("x") * lax.axis_size("c")
    array = jax.ShapeDtypeStruct
    place = jnp.stack([core, lax.axis_index("yl"), lax.axis_index(("yh", "x", "c")), lax.axis_index("z")]).astype(i32)

    (block,) = call(pack_kernel, (array((ring, rows + PACK, width), bf16),), 3, away=(0,), nbytes=2 * MIB)(
        place, points, membership.reshape(1, rows)
    )
    spread = lax.all_to_all(block, "z", 0, 0)

    landmarks = landmark_pool[landmark_ids]

    def load(which):
        return jnp.concatenate(
            [lax.dynamic_slice_in_dim(m, which * quarter, quarter, 0) for m in (landmarks, whitening)]
        )

    up = hop(load(2 * core), ("yh", "yl"), 1)
    down = hop(load(2 * core + 1), ("yh", "yl"), -1)
    up_o, down_o = flip(up, "c", 1), flip(down, "c", 1)
    pieces = (up, down, up_o, down_o)

    kernel, keep, send = call(
        functools.partial(affinity_kernel, rows),
        (
            array((ring * rows, 2 * count), bf16),
            array((half, 2 * count + TALLY), bf16),
            array((half, 2 * count + TALLY), bf16),
        ),
        7,
        5,
        [pltpu.VMEM((clusters, ring * rows), bf16)] + store(2 * count, width),
        flops=2 * ring * rows * 2 * count * (width + clusters),
        nbytes=6 * MIB,
    )(place, spread, landmarks, *pieces)

    theirs = flip(send, "c", 1)
    token = array((8, 128), f32)

    leave, stay, done = call(
        functools.partial(project_kernel, rows),
        (array((ring // 2 * rows, rank_width), bf16), array((ring // 2 * rows, rank_width), bf16), token),
        7,
        5,
        store(2 * count, rank_width),
        away=(0, 1),
        flops=2 * ring * rows * 2 * count * rank_width,
        nbytes=3 * MIB,
    )(place, kernel, whitening, *pieces)
    (paired,) = call(pair_kernel, (array(keep.shape, bf16),), 4, away=(0,), nbytes=2 * MIB)(place, keep, theirs, done)
    gathered = lax.all_to_all(paired.reshape(peers, share, -1), PLANE, 0, 0)

    def merge(kept, leave, partner):
        size = array((kept.shape[0] // 2, rank_width), bf16)
        arrived = flip(leave, "z", partner)
        return call(merge_kernel, (size, size, token), 3, away=(0, 1), nbytes=MIB)(place, kept, arrived)

    kept, leave, done = merge(stay, leave, 1)
    mapped, number = call(
        cluster_kernel,
        (array((ring, share, rank_width), f32), array((share, rank_width), f32)),
        8,
        5,
        store(2 * count, rank_width),
        away=(0,),
        nbytes=3 * MIB,
    )(place, gathered, done, whitening, *pieces)
    over = lax.all_to_all(mapped, "z", 0, 0)
    kept, leave, done = merge(kept, leave, 3)
    (sent,) = call(means_kernel, (array((peers, share, rank_width), bf16),), 4, away=(0,), nbytes=MIB)(
        place, over, number, done
    )
    mine = lax.all_to_all(sent, PLANE, 0, 0).reshape(half, rank_width)
    last = flip(leave, "z", 7)
    features, choose, mine = call(
        feature_kernel,
        (
            array((rows, rank_width), bf16),
            array((clusters // groups, clusters), bf16),
            array((half, rank_width), bf16),
        ),
        5,
        nbytes=2 * MIB,
    )(place, owner_map.reshape(1, clusters), mine, kept, last)
    other = flip(mine, "c", 1)
    near_scores, near_owned = call(
        near_kernel, (array((rows, half), f32), array((clusters // groups, rank_width), f32)), 4, nbytes=MIB
    )(place, features, mine, choose)
    scores, owned = call(
        far_kernel, (array((rows, clusters), f32), array((clusters // groups, rank_width), bf16)), 6, nbytes=MIB
    )(place, features, other, choose, near_scores, near_owned)
    return (features, owned, scores)


def build(mesh, factors):
    fine = Mesh(mesh.devices.reshape(factors), ALL)
    blk, dp = ("z", "yl"), ("yh", "x", "c")
    return jax.shard_map(
        body,
        mesh=fine,
        in_specs=(P(ALL, None), P(ALL), P(blk, None), P(blk), P(blk, None), P()),
        out_specs=(P(ALL, None), P(dp, None), P(ALL, None)),
        check_vma=False,
    )


def solution(mesh):
    return build(mesh, (4, 4, 2, 8, 2))
```

```python
import functools
import math

import jax
import jax.numpy as jnp
from jax import lax
from jax.experimental import pallas as pl
from jax.experimental.pallas import tpu as pltpu
from jax.sharding import Mesh, PartitionSpec as P

epsilon = 1e-06
bf16 = jnp.bfloat16
f32 = jnp.float32
i32 = jnp.int32
ALL = ("yh", "x", "c", "z", "yl")
PLANE = ("yh", "x", "yl")
PACK = 8
LEAVE = (1, 6, 2, 5)
STAY = (0, 7, 3, 4)
DIGIT = 128
TALLY = 128
MIB = 1 << 20


def hop(value, axis, by):
    size = math.prod(lax.axis_size(name) for name in axis)
    return lax.ppermute(value, axis, [(i, (i + by) % size) for i in range(size)])


def flip(value, axis, bit):
    size = lax.axis_size(axis)
    return lax.ppermute(value, axis, [(i, i ^ bit) for i in range(size)])


def across(a, b):
    return lax.dot_general(a, b, (((1,), (1,)), ((), ())), preferred_element_type=f32)


def call(kernel, out, ins, held=0, scratch=(), away=(), pinned=(), flops=0, nbytes=0):
    spec = pl.BlockSpec(memory_space=pltpu.VMEM)
    far = pl.BlockSpec(memory_space=pltpu.HBM)
    scratch, many = list(scratch), len(out)
    own = len(scratch)
    for i in away:
        scratch += [pltpu.VMEM(out[i].shape, out[i].dtype), pltpu.SemaphoreType.DMA]

    def run(*refs):
        outs, extra = list(refs[ins : ins + many]), refs[ins + many :]
        moves = []
        for n, i in enumerate(away):
            staged, sem = extra[own + 2 * n : own + 2 * n + 2]
            moves.append(pltpu.make_async_copy(staged, outs[i], sem))
            outs[i] = staged
        kernel(*refs[:ins], *outs, *extra[:own])
        for move in moves:
            move.start()
        for move in moves:
            move.wait()

    made = pl.pallas_call(
        run,
        out_shape=tuple(
            pltpu.HBM(o.shape, o.dtype) if i in away else pltpu.VMEM(o.shape, o.dtype) if i in pinned else o
            for i, o in enumerate(out)
        ),
        in_specs=[pl.BlockSpec(memory_space=pltpu.SMEM)] + [spec] * (ins - 1 - held) + [far] * held,
        out_specs=tuple(far if i in away else spec for i in range(many)),
        scratch_shapes=scratch,
        compiler_params=pltpu.CompilerParams(vmem_limit_bytes=16 * MIB),
        cost_estimate=pl.CostEstimate(flops=flops, bytes_accessed=nbytes, transcendentals=0),
    )
    near = ins - held
    return lambda *args: made(*args[:near], *(pltpu.with_memory_space_constraint(a, pltpu.HBM) for a in args[near:]))


def fetch(place, block, swapped, second, table, sems):
    core, half = place[0], place[1]
    count = block.shape[0]
    quarter = count // 4
    copies = [pltpu.make_async_copy(block, table.at[pl.ds(pl.multiple_of(half * count, count), count), :], sems.at[0])]
    for i, piece in enumerate(swapped):
        which = core if i < 2 else 1 - core
        at = pl.multiple_of((1 - half) * count + (2 * which + i % 2) * quarter, quarter)
        source = piece.at[pl.ds(second * quarter, quarter), :]
        copies.append(pltpu.make_async_copy(source, table.at[pl.ds(at, quarter), :], sems.at[1 + i]))
    for copy in copies:
        copy.start()
    return copies


def store(count, width):
    return [pltpu.VMEM((count, width), bf16), pltpu.SemaphoreType.DMA((5,))]


def row_squares(matrix):
    column = jnp.sum(jnp.square(matrix.astype(f32)), axis=1, keepdims=True)
    return jnp.broadcast_to(column, (matrix.shape[0], 128)).T[0:1]


def pack_kernel(place, points, members, out):
    rows, width = points.shape
    code = jnp.broadcast_to(members[...], (PACK, rows))
    row = lax.broadcasted_iota(i32, (PACK, rows), 0)
    digits = jnp.where(row == 0, code // DIGIT, jnp.where(row == 1, code % DIGIT, 0)).astype(f32).astype(bf16)
    lane = lax.broadcasted_iota(i32, (rows, width), 1) - place[3] * rows
    spot = jnp.where(lane == lax.broadcasted_iota(i32, (rows, width), 0), 1.0, 0.0).astype(bf16)
    tail = jnp.dot(digits, spot, preferred_element_type=f32).astype(bf16)
    for i in range(out.shape[0]):
        out[i, :rows, :] = points[...]
        out[i, rows:, :] = tail


def affinity_kernel(
    rows, place, came, own, up, down, up_o, down_o, kernel, keep, send, table, spread, arrival, anchors, sems
):
    first = pltpu.make_async_copy(came, spread, arrival)
    first.start()
    copies = fetch(place, own, (up, down, up_o, down_o), 0, anchors, sems)
    first.wait()
    core = place[0]
    ring, _, width = spread.shape
    half = keep.shape[0]
    count = anchors.shape[0]
    points = ring * rows
    codes = jnp.sum(spread[:, rows:, :].astype(f32), axis=0)
    members = (codes[0:1, :points] * DIGIT + codes[1:2, :points]).astype(i32)
    label = lax.broadcasted_iota(i32, (half, points), 0)
    for ref, part in ((keep, 0), (send, 1)):
        which = jnp.where(core == 0, part, 1 - part)
        hit = jnp.where(label + which * half == members, 1.0, 0.0)
        table[part * half : (part + 1) * half, :] = hit.astype(bf16)
        tally = jnp.sum(hit, axis=1, keepdims=True)
        big = jnp.floor(tally * (1.0 / DIGIT))
        lane = lax.broadcasted_iota(i32, (half, TALLY), 1)
        digits = jnp.where(lane == 0, big, jnp.where(lane == 1, tally - big * DIGIT, 0.0))
        ref[:, count:] = digits.astype(bf16)
    visitors = spread[:, :rows, :].reshape(points, width)
    length = lax.rsqrt(jnp.sum(jnp.square(visitors.astype(f32)), axis=1, keepdims=True) + epsilon) * math.sqrt(width)
    for copy in copies:
        copy.wait()
    tile = min(256, count)

    for at in range(0, count, tile):
        values = spread[:, :rows, :].reshape(points, width)
        marks = anchors[pl.ds(at, tile), :]
        factor = lax.rsqrt(row_squares(marks) + epsilon)
        part = jnp.exp(across(values, marks) * length * factor).astype(bf16)
        kernel[:, pl.ds(at, tile)] = part
        sums = jnp.dot(table[...], part, preferred_element_type=f32).astype(bf16)
        keep[:, pl.ds(at, tile)] = sums[:half]
        send[:, pl.ds(at, tile)] = sums[half:]


def project(place, kernel, maps, owners, rows, at, tile):
    spots = [pl.multiple_of(lax.bitwise_xor(place[3], d) * rows, rows) for d in owners]
    span = jnp.concatenate([kernel[pl.ds(spot, rows), :] for spot in spots])
    return jnp.dot(span, maps[:, pl.ds(at, tile)], preferred_element_type=f32)


def leave_kernel(rows, place, kernel, white, up, down, up_o, down_o, leave, token, maps, sems):
    copies = fetch(place, white, (up, down, up_o, down_o), 1, maps, sems)
    for copy in copies:
        copy.wait()
    token[...] = jnp.zeros_like(token)
    tile = min(256, leave.shape[1])
    for at in range(0, leave.shape[1], tile):
        leave[:, at : at + tile] = project(place, kernel, maps, LEAVE, rows, at, tile).astype(bf16)


def stay_kernel(rows, place, kernel, white, up, down, up_o, down_o, stay, maps, sems):
    for copy in fetch(place, white, (up, down, up_o, down_o), 1, maps, sems):
        copy.wait()
    tile = min(256, stay.shape[1])
    for at in range(0, stay.shape[1], tile):
        stay[:, at : at + tile] = project(place, kernel, maps, STAY, rows, at, tile).astype(bf16)


def merge_kernel(place, kept, arrived, keep, send, token):
    half = keep.shape[0]
    both = (kept[...].astype(f32) + arrived[...].astype(f32)).astype(bf16)
    keep[...] = both[:half]
    send[...] = both[half:]
    token[...] = jnp.zeros_like(token)


def cluster_kernel(place, spread, _, white, up, down, up_o, down_o, mapped, number, maps, sems):
    copies = fetch(place, white, (up, down, up_o, down_o), 1, maps, sems)
    count = maps.shape[0]
    share = spread.shape[1]
    total = jnp.sum(spread[...].astype(f32), axis=0)
    sums = total[:, :count]
    high = sums.astype(bf16).astype(f32)
    both = jnp.concatenate([high, sums - high]).astype(bf16)
    tally = total[:, count : count + 1] * DIGIT + total[:, count + 1 : count + 2]
    number[...] = jnp.broadcast_to(jnp.maximum(tally, 1.0), number.shape)
    for copy in copies:
        copy.wait()
    result = jnp.dot(both, maps[...], preferred_element_type=f32)
    mapped[...] = jnp.broadcast_to((result[:share] + result[share:])[None], mapped.shape)


def pair_kernel(place, keep, theirs, _, paired):
    paired[...] = (keep[...].astype(f32) + theirs[...].astype(f32)).astype(bf16)


def means_kernel(place, parts, number, _, sent):
    means = jnp.sum(parts[...], axis=0) / number[...]
    sent[...] = jnp.broadcast_to(means[None], sent.shape).astype(bf16)


def feature_kernel(place, owners, *rest):
    kept, last, features, again, choose = rest
    both = (kept[...].astype(f32) + last[...].astype(f32)).astype(bf16)
    features[...] = both
    again[...] = both
    slots, clusters = choose.shape
    owned = owners[...] == place[2]
    row = lax.broadcasted_iota(i32, (clusters, clusters), 0)
    col = lax.broadcasted_iota(i32, (clusters, clusters), 1)
    before = jnp.where(row < col, 1.0, 0.0).astype(bf16)
    mark = jnp.broadcast_to(jnp.where(owned, 1.0, 0.0), (slots, clusters))
    rank = jnp.dot(mark.astype(bf16), before, preferred_element_type=f32)
    slot = lax.broadcasted_iota(i32, (slots, clusters), 0).astype(f32)
    choose[...] = jnp.where(rank == slot, mark, 0.0).astype(bf16)


def after_kernel(place, means, _, same):
    same[...] = means[...]


def half_scores(features, means, choose, at):
    half = means.shape[0]
    norms = row_squares(means[...])
    scores = (norms - 2.0 * across(features[...], means[...])) * (1.0 / means.shape[1])
    owned = jnp.dot(choose[:, pl.ds(at, half)], means[...], preferred_element_type=f32)
    return scores, owned


def near_kernel(place, features, means, choose, scores, owned):
    half = means.shape[0]
    at = pl.multiple_of(place[0] * half, half)
    scores[...], owned[...] = half_scores(features, means, choose, at)


def far_kernel(place, features, means, choose, near_scores, near_owned, scores, owned):
    half = means.shape[0]
    there = pl.multiple_of((1 - place[0]) * half, half)
    here = pl.multiple_of(place[0] * half, half)
    far, rest = half_scores(features, means, choose, there)
    scores[:, pl.ds(there, half)] = far
    scores[:, pl.ds(here, half)] = near_scores[...]
    owned[...] = (near_owned[...] + rest).astype(bf16)


def body(points, membership, landmark_pool, landmark_ids, whitening, owner_map):
    rows, width = points.shape
    count, rank_width = whitening.shape
    clusters = owner_map.shape[0]
    ring = lax.axis_size("z")
    core = lax.axis_index("c")
    quarter = count // 4
    half = clusters // 2
    peers = math.prod(lax.axis_size(name) for name in PLANE)
    share = half // peers
    groups = lax.axis_size("yh") * lax.axis_size("x") * lax.axis_size("c")
    array = jax.ShapeDtypeStruct
    place = jnp.stack([core, lax.axis_index("yl"), lax.axis_index(("yh", "x", "c")), lax.axis_index("z")]).astype(i32)

    (block,) = call(pack_kernel, (array((ring, rows + PACK, width), bf16),), 3, 0, away=(0,), nbytes=2 * MIB)(
        place, points, membership.reshape(1, rows)
    )
    spread = lax.all_to_all(block, "z", 0, 0)

    landmarks = landmark_pool[landmark_ids]

    def load(which):
        return jnp.concatenate(
            [lax.dynamic_slice_in_dim(m, which * quarter, quarter, 0) for m in (landmarks, whitening)]
        )

    up = hop(load(2 * core), ("yh", "yl"), 1)
    down = hop(load(2 * core + 1), ("yh", "yl"), -1)
    up_o, down_o = flip(up, "c", 1), flip(down, "c", 1)
    pieces = (up, down, up_o, down_o)

    kernel, keep, send = call(
        functools.partial(affinity_kernel, rows),
        (
            array((ring * rows, 2 * count), bf16),
            array((half, 2 * count + TALLY), bf16),
            array((half, 2 * count + TALLY), bf16),
        ),
        7,
        6,
        [
            pltpu.VMEM((clusters, ring * rows), bf16),
            pltpu.VMEM(spread.shape, bf16),
            pltpu.SemaphoreType.DMA,
            *store(2 * count, width),
        ],
        flops=2 * ring * rows * 2 * count * (width + clusters),
        nbytes=6 * MIB,
    )(place, spread, landmarks, *pieces)

    theirs = flip(send, "c", 1)
    token = array((8, 128), f32)

    leave, done = call(
        functools.partial(leave_kernel, rows),
        (array((ring // 2 * rows, rank_width), bf16), token),
        7,
        5,
        store(2 * count, rank_width),
        away=(0,),
        flops=ring * rows * 2 * count * rank_width,
        nbytes=3 * MIB,
    )(place, kernel, whitening, *pieces)
    (paired,) = call(pair_kernel, (array(keep.shape, bf16),), 4, away=(0,), nbytes=2 * MIB)(place, keep, theirs, done)
    gathered = lax.all_to_all(paired.reshape(peers, share, -1), PLANE, 0, 0)

    def merge(kept, leave, partner):
        size = array((kept.shape[0] // 2, rank_width), bf16)
        arrived = flip(leave, "z", partner)
        return call(merge_kernel, (size, size, token), 3, away=(0, 1), nbytes=MIB)(place, kept, arrived)

    (stay,) = call(
        functools.partial(stay_kernel, rows),
        (array((ring // 2 * rows, rank_width), bf16),),
        7,
        5,
        store(2 * count, rank_width),
        flops=ring * rows * 2 * count * rank_width,
        nbytes=3 * MIB,
    )(place, kernel, whitening, *pieces)
    kept, leave, done = merge(stay, leave, 1)
    mapped, number = call(
        cluster_kernel,
        (array((ring, share, rank_width), f32), array((share, rank_width), f32)),
        8,
        5,
        store(2 * count, rank_width),
        away=(0,),
        nbytes=3 * MIB,
    )(place, gathered, done, whitening, *pieces)
    over = lax.all_to_all(mapped, "z", 0, 0)
    kept, leave, done = merge(kept, leave, 3)
    (sent,) = call(means_kernel, (array((peers, share, rank_width), bf16),), 4, away=(0,), nbytes=MIB)(
        place, over, number, done
    )
    mine = lax.all_to_all(sent, PLANE, 0, 0).reshape(half, rank_width)
    last = flip(leave, "z", 7)
    features, again, choose = call(
        feature_kernel,
        (
            array((rows, rank_width), bf16),
            array((rows, rank_width), bf16),
            array((clusters // groups, clusters), bf16),
        ),
        4,
        pinned=(1,),
        nbytes=2 * MIB,
    )(place, owner_map.reshape(1, clusters), kept, last)
    (mine,) = call(after_kernel, (array(mine.shape, bf16),), 3, nbytes=MIB)(place, mine, choose)
    other = flip(mine, "c", 1)
    near_scores, near_owned = call(
        near_kernel, (array((rows, half), f32), array((clusters // groups, rank_width), f32)), 4, nbytes=MIB
    )(place, again, mine, choose)
    scores, owned = call(
        far_kernel, (array((rows, clusters), f32), array((clusters // groups, rank_width), bf16)), 6, nbytes=MIB
    )(place, again, other, choose, near_scores, near_owned)
    return (features, owned, scores)


def build(mesh, factors):
    fine = Mesh(mesh.devices.reshape(factors), ALL)
    blk, dp = ("z", "yl"), ("yh", "x", "c")
    return jax.shard_map(
        body,
        mesh=fine,
        in_specs=(P(ALL, None), P(ALL), P(blk, None), P(blk), P(blk, None), P()),
        out_specs=(P(ALL, None), P(dp, None), P(ALL, None)),
        check_vma=False,
    )


def solution(mesh):
    return build(mesh, (4, 4, 2, 8, 2))
```

```python
import functools
import math

import jax
import jax.numpy as jnp
from jax import lax
from jax.experimental import pallas as pl
from jax.experimental.pallas import tpu as pltpu
from jax.sharding import Mesh, PartitionSpec as P

epsilon = 1e-06
bf16 = jnp.bfloat16
f32 = jnp.float32
i32 = jnp.int32
ALL = ("yh", "x", "c", "z", "yl")
PLANE = ("yh", "x", "yl")
PACK = 8
LEAVE = (1, 6, 2, 5)
STAY = (0, 7, 3, 4)
DIGIT = 128
TALLY = 128
MIB = 1 << 20


def hop(value, axis, by):
    size = math.prod(lax.axis_size(name) for name in axis)
    return lax.ppermute(value, axis, [(i, (i + by) % size) for i in range(size)])


def flip(value, axis, bit):
    size = lax.axis_size(axis)
    return lax.ppermute(value, axis, [(i, i ^ bit) for i in range(size)])


def across(a, b):
    return lax.dot_general(a, b, (((1,), (1,)), ((), ())), preferred_element_type=f32)


def call(kernel, out, ins, held=0, scratch=(), away=(), pinned=(), flops=0, nbytes=0):
    spec = pl.BlockSpec(memory_space=pltpu.VMEM)
    far = pl.BlockSpec(memory_space=pltpu.HBM)
    scratch, many = list(scratch), len(out)
    own = len(scratch)
    for i in away:
        scratch += [pltpu.VMEM(out[i].shape, out[i].dtype), pltpu.SemaphoreType.DMA]

    def run(*refs):
        outs, extra = list(refs[ins : ins + many]), refs[ins + many :]
        moves = []
        for n, i in enumerate(away):
            staged, sem = extra[own + 2 * n : own + 2 * n + 2]
            moves.append(pltpu.make_async_copy(staged, outs[i], sem))
            outs[i] = staged
        kernel(*refs[:ins], *outs, *extra[:own])
        for move in moves:
            move.start()
        for move in moves:
            move.wait()

    made = pl.pallas_call(
        run,
        out_shape=tuple(
            pltpu.HBM(o.shape, o.dtype) if i in away else pltpu.VMEM(o.shape, o.dtype) if i in pinned else o
            for i, o in enumerate(out)
        ),
        in_specs=[pl.BlockSpec(memory_space=pltpu.SMEM)] + [spec] * (ins - 1 - held) + [far] * held,
        out_specs=tuple(far if i in away else spec for i in range(many)),
        scratch_shapes=scratch,
        compiler_params=pltpu.CompilerParams(vmem_limit_bytes=16 * MIB),
        cost_estimate=pl.CostEstimate(flops=flops, bytes_accessed=nbytes, transcendentals=0),
    )
    near = ins - held
    return lambda *args: made(*args[:near], *(pltpu.with_memory_space_constraint(a, pltpu.HBM) for a in args[near:]))


def fetch(place, block, swapped, second, table, sems):
    core, half = place[0], place[1]
    count = block.shape[0]
    quarter = count // 4
    copies = [pltpu.make_async_copy(block, table.at[pl.ds(pl.multiple_of(half * count, count), count), :], sems.at[0])]
    for i, piece in enumerate(swapped):
        which = core if i < 2 else 1 - core
        at = pl.multiple_of((1 - half) * count + (2 * which + i % 2) * quarter, quarter)
        source = piece.at[pl.ds(second * quarter, quarter), :]
        copies.append(pltpu.make_async_copy(source, table.at[pl.ds(at, quarter), :], sems.at[1 + i]))
    for copy in copies:
        copy.start()
    return copies


def store(count, width):
    return [pltpu.VMEM((count, width), bf16), pltpu.SemaphoreType.DMA((5,))]


def row_squares(matrix):
    column = jnp.sum(jnp.square(matrix.astype(f32)), axis=1, keepdims=True)
    return jnp.broadcast_to(column, (matrix.shape[0], 128)).T[0:1]


def pack_kernel(place, given, marked, out, points, members, sems):
    copies = [pltpu.make_async_copy(given, points, sems.at[0]), pltpu.make_async_copy(marked, members, sems.at[1])]
    for copy in copies:
        copy.start()
    for copy in copies:
        copy.wait()
    rows, width = points.shape
    code = jnp.broadcast_to(members[...], (PACK, rows))
    row = lax.broadcasted_iota(i32, (PACK, rows), 0)
    digits = jnp.where(row == 0, code // DIGIT, jnp.where(row == 1, code % DIGIT, 0)).astype(f32).astype(bf16)
    lane = lax.broadcasted_iota(i32, (rows, width), 1) - place[3] * rows
    spot = jnp.where(lane == lax.broadcasted_iota(i32, (rows, width), 0), 1.0, 0.0).astype(bf16)
    tail = jnp.dot(digits, spot, preferred_element_type=f32).astype(bf16)
    for i in range(out.shape[0]):
        out[i, :rows, :] = points[...]
        out[i, rows:, :] = tail


def affinity_kernel(
    rows, place, came, own, up, down, up_o, down_o, kernel, keep, send, table, spread, arrival, anchors, sems
):
    first = pltpu.make_async_copy(came, spread, arrival)
    first.start()
    copies = fetch(place, own, (up, down, up_o, down_o), 0, anchors, sems)
    first.wait()
    core = place[0]
    ring, _, width = spread.shape
    half = keep.shape[0]
    count = anchors.shape[0]
    points = ring * rows
    codes = jnp.sum(spread[:, rows:, :].astype(f32), axis=0)
    members = (codes[0:1, :points] * DIGIT + codes[1:2, :points]).astype(i32)
    label = lax.broadcasted_iota(i32, (half, points), 0)
    for ref, part in ((keep, 0), (send, 1)):
        which = jnp.where(core == 0, part, 1 - part)
        hit = jnp.where(label + which * half == members, 1.0, 0.0)
        table[part * half : (part + 1) * half, :] = hit.astype(bf16)
        tally = jnp.sum(hit, axis=1, keepdims=True)
        big = jnp.floor(tally * (1.0 / DIGIT))
        lane = lax.broadcasted_iota(i32, (half, TALLY), 1)
        digits = jnp.where(lane == 0, big, jnp.where(lane == 1, tally - big * DIGIT, 0.0))
        ref[:, count:] = digits.astype(bf16)
    visitors = spread[:, :rows, :].reshape(points, width)
    length = lax.rsqrt(jnp.sum(jnp.square(visitors.astype(f32)), axis=1, keepdims=True) + epsilon) * math.sqrt(width)
    for copy in copies:
        copy.wait()
    tile = min(256, count)

    for at in range(0, count, tile):
        values = spread[:, :rows, :].reshape(points, width)
        marks = anchors[pl.ds(at, tile), :]
        factor = lax.rsqrt(row_squares(marks) + epsilon)
        part = jnp.exp(across(values, marks) * length * factor).astype(bf16)
        kernel[:, pl.ds(at, tile)] = part
        sums = jnp.dot(table[...], part, preferred_element_type=f32).astype(bf16)
        keep[:, pl.ds(at, tile)] = sums[:half]
        send[:, pl.ds(at, tile)] = sums[half:]


def project(place, kernel, maps, owners, rows, at, tile):
    spots = [pl.multiple_of(lax.bitwise_xor(place[3], d) * rows, rows) for d in owners]
    span = jnp.concatenate([kernel[pl.ds(spot, rows), :] for spot in spots])
    return jnp.dot(span, maps[:, pl.ds(at, tile)], preferred_element_type=f32)


def leave_kernel(rows, place, kernel, white, up, down, up_o, down_o, leave, token, maps, sems):
    copies = fetch(place, white, (up, down, up_o, down_o), 1, maps, sems)
    for copy in copies:
        copy.wait()
    token[...] = jnp.zeros_like(token)
    tile = min(256, leave.shape[1])
    for at in range(0, leave.shape[1], tile):
        leave[:, at : at + tile] = project(place, kernel, maps, LEAVE, rows, at, tile).astype(bf16)


def stay_kernel(rows, place, kernel, white, up, down, up_o, down_o, stay, maps, sems):
    for copy in fetch(place, white, (up, down, up_o, down_o), 1, maps, sems):
        copy.wait()
    tile = min(256, stay.shape[1])
    for at in range(0, stay.shape[1], tile):
        stay[:, at : at + tile] = project(place, kernel, maps, STAY, rows, at, tile).astype(bf16)


def merge_kernel(place, kept, arrived, keep, send, token):
    half = keep.shape[0]
    both = (kept[...].astype(f32) + arrived[...].astype(f32)).astype(bf16)
    keep[...] = both[:half]
    send[...] = both[half:]
    token[...] = jnp.zeros_like(token)


def cluster_kernel(place, spread, _, white, up, down, up_o, down_o, mapped, number, maps, sems):
    copies = fetch(place, white, (up, down, up_o, down_o), 1, maps, sems)
    count = maps.shape[0]
    share = spread.shape[1]
    total = jnp.sum(spread[...].astype(f32), axis=0)
    sums = total[:, :count]
    high = sums.astype(bf16).astype(f32)
    both = jnp.concatenate([high, sums - high]).astype(bf16)
    tally = total[:, count : count + 1] * DIGIT + total[:, count + 1 : count + 2]
    number[...] = jnp.broadcast_to(jnp.maximum(tally, 1.0), number.shape)
    for copy in copies:
        copy.wait()
    result = jnp.dot(both, maps[...], preferred_element_type=f32)
    mapped[...] = jnp.broadcast_to((result[:share] + result[share:])[None], mapped.shape)


def pair_kernel(place, keep, theirs, _, paired):
    paired[...] = (keep[...].astype(f32) + theirs[...].astype(f32)).astype(bf16)


def means_kernel(place, parts, number, sent):
    means = jnp.sum(parts[...], axis=0) / number[...]
    sent[...] = jnp.broadcast_to(means[None], sent.shape).astype(bf16)


def feature_kernel(place, owners, *rest):
    kept, last, features, again, choose = rest
    both = (kept[...].astype(f32) + last[...].astype(f32)).astype(bf16)
    features[...] = both
    again[...] = both
    slots, clusters = choose.shape
    owned = owners[...] == place[2]
    row = lax.broadcasted_iota(i32, (clusters, clusters), 0)
    col = lax.broadcasted_iota(i32, (clusters, clusters), 1)
    before = jnp.where(row < col, 1.0, 0.0).astype(bf16)
    mark = jnp.broadcast_to(jnp.where(owned, 1.0, 0.0), (slots, clusters))
    rank = jnp.dot(mark.astype(bf16), before, preferred_element_type=f32)
    slot = lax.broadcasted_iota(i32, (slots, clusters), 0).astype(f32)
    choose[...] = jnp.where(rank == slot, mark, 0.0).astype(bf16)


def after_kernel(place, means, _, same):
    same[...] = means[...]


def half_scores(features, means, choose, at):
    half = means.shape[0]
    norms = row_squares(means[...])
    scores = (norms - 2.0 * across(features[...], means[...])) * (1.0 / means.shape[1])
    owned = jnp.dot(choose[:, pl.ds(at, half)], means[...], preferred_element_type=f32)
    return scores, owned


def near_kernel(place, features, means, choose, scores, owned):
    half = means.shape[0]
    at = pl.multiple_of(place[0] * half, half)
    scores[...], owned[...] = half_scores(features, means, choose, at)


def far_kernel(place, features, means, choose, near_scores, near_owned, scores, owned):
    half = means.shape[0]
    there = pl.multiple_of((1 - place[0]) * half, half)
    here = pl.multiple_of(place[0] * half, half)
    far, rest = half_scores(features, means, choose, there)
    scores[:, pl.ds(there, half)] = far
    scores[:, pl.ds(here, half)] = near_scores[...]
    owned[...] = (near_owned[...] + rest).astype(bf16)


def body(points, membership, landmark_pool, landmark_ids, whitening, owner_map):
    rows, width = points.shape
    count, rank_width = whitening.shape
    clusters = owner_map.shape[0]
    ring = lax.axis_size("z")
    core = lax.axis_index("c")
    quarter = count // 4
    half = clusters // 2
    peers = math.prod(lax.axis_size(name) for name in PLANE)
    share = half // peers
    groups = lax.axis_size("yh") * lax.axis_size("x") * lax.axis_size("c")
    array = jax.ShapeDtypeStruct
    place = jnp.stack([core, lax.axis_index("yl"), lax.axis_index(("yh", "x", "c")), lax.axis_index("z")]).astype(i32)

    (block,) = call(
        pack_kernel,
        (array((ring, rows + PACK, width), bf16),),
        3,
        2,
        [pltpu.VMEM((rows, width), bf16), pltpu.VMEM((1, rows), i32), pltpu.SemaphoreType.DMA((2,))],
        away=(0,),
        nbytes=2 * MIB,
    )(place, points, membership.reshape(1, rows))
    spread = lax.all_to_all(block, "z", 0, 0)

    landmarks = landmark_pool[landmark_ids]

    def load(which):
        return jnp.concatenate(
            [lax.dynamic_slice_in_dim(m, which * quarter, quarter, 0) for m in (landmarks, whitening)]
        )

    up = hop(load(2 * core), ("yh", "yl"), 1)
    down = hop(load(2 * core + 1), ("yh", "yl"), -1)
    up_o, down_o = flip(up, "c", 1), flip(down, "c", 1)
    pieces = (up, down, up_o, down_o)

    kernel, keep, send = call(
        functools.partial(affinity_kernel, rows),
        (
            array((ring * rows, 2 * count), bf16),
            array((half, 2 * count + TALLY), bf16),
            array((half, 2 * count + TALLY), bf16),
        ),
        7,
        6,
        [
            pltpu.VMEM((clusters, ring * rows), bf16),
            pltpu.VMEM(spread.shape, bf16),
            pltpu.SemaphoreType.DMA,
            *store(2 * count, width),
        ],
        flops=2 * ring * rows * 2 * count * (width + clusters),
        nbytes=6 * MIB,
    )(place, spread, landmarks, *pieces)

    theirs = flip(send, "c", 1)
    token = array((8, 128), f32)

    leave, done = call(
        functools.partial(leave_kernel, rows),
        (array((ring // 2 * rows, rank_width), bf16), token),
        7,
        5,
        store(2 * count, rank_width),
        away=(0,),
        flops=ring * rows * 2 * count * rank_width,
        nbytes=3 * MIB,
    )(place, kernel, whitening, *pieces)
    (paired,) = call(pair_kernel, (array(keep.shape, bf16),), 4, away=(0,), nbytes=2 * MIB)(place, keep, theirs, done)
    gathered = lax.all_to_all(paired.reshape(peers, share, -1), PLANE, 0, 0)

    def merge(kept, leave, partner):
        size = array((kept.shape[0] // 2, rank_width), bf16)
        arrived = flip(leave, "z", partner)
        return call(merge_kernel, (size, size, token), 3, away=(0, 1), nbytes=MIB)(place, kept, arrived)

    (stay,) = call(
        functools.partial(stay_kernel, rows),
        (array((ring // 2 * rows, rank_width), bf16),),
        7,
        5,
        store(2 * count, rank_width),
        flops=64 * ring * rows * 2 * count * rank_width,
        nbytes=3 * MIB,
    )(place, kernel, whitening, *pieces)
    kept, leave, _ = merge(stay, leave, 1)
    kept, leave, done = merge(kept, leave, 3)
    mapped, number = call(
        cluster_kernel,
        (array((ring, share, rank_width), f32), array((share, rank_width), f32)),
        8,
        5,
        store(2 * count, rank_width),
        away=(0,),
        nbytes=3 * MIB,
    )(place, gathered, done, whitening, *pieces)
    over = lax.all_to_all(mapped, "z", 0, 0)
    (sent,) = call(means_kernel, (array((peers, share, rank_width), bf16),), 3, away=(0,), nbytes=MIB)(
        place, over, number
    )
    mine = lax.all_to_all(sent, PLANE, 0, 0).reshape(half, rank_width)
    last = flip(leave, "z", 7)
    features, again, choose = call(
        feature_kernel,
        (
            array((rows, rank_width), bf16),
            array((rows, rank_width), bf16),
            array((clusters // groups, clusters), bf16),
        ),
        4,
        pinned=(1,),
        nbytes=2 * MIB,
    )(place, owner_map.reshape(1, clusters), kept, last)
    (mine,) = call(after_kernel, (array(mine.shape, bf16),), 3, nbytes=MIB)(place, mine, choose)
    other = flip(mine, "c", 1)
    near_scores, near_owned = call(
        near_kernel, (array((rows, half), f32), array((clusters // groups, rank_width), f32)), 4, nbytes=MIB
    )(place, again, mine, choose)
    scores, owned = call(
        far_kernel, (array((rows, clusters), f32), array((clusters // groups, rank_width), bf16)), 6, nbytes=MIB
    )(place, again, other, choose, near_scores, near_owned)
    return (features, owned, scores)


def build(mesh, factors):
    fine = Mesh(mesh.devices.reshape(factors), ALL)
    blk, dp = ("z", "yl"), ("yh", "x", "c")
    return jax.shard_map(
        body,
        mesh=fine,
        in_specs=(P(ALL, None), P(ALL), P(blk, None), P(blk), P(blk, None), P()),
        out_specs=(P(ALL, None), P(dp, None), P(ALL, None)),
        check_vma=False,
    )


def solution(mesh):
    return build(mesh, (4, 4, 2, 8, 2))
```

```python
import functools
import math

import jax
import jax.numpy as jnp
from jax import lax
from jax.experimental import pallas as pl
from jax.experimental.pallas import tpu as pltpu
from jax.sharding import Mesh, PartitionSpec as P

epsilon = 1e-06
bf16 = jnp.bfloat16
f32 = jnp.float32
i32 = jnp.int32
ALL = ("yh", "x", "c", "z", "yl")
PLANE = ("yh", "x", "yl")
PACK = 8
LONG = 1 << 36
LEAVE = (1, 6, 2, 5)
STAY = (0, 7, 3, 4)
DIGIT = 128
TALLY = 128
MIB = 1 << 20


def hop(value, axis, by):
    size = math.prod(lax.axis_size(name) for name in axis)
    return lax.ppermute(value, axis, [(i, (i + by) % size) for i in range(size)])


def flip(value, axis, bit):
    size = lax.axis_size(axis)
    return lax.ppermute(value, axis, [(i, i ^ bit) for i in range(size)])


def across(a, b):
    return lax.dot_general(a, b, (((1,), (1,)), ((), ())), preferred_element_type=f32)


def call(kernel, out, ins, held=0, scratch=(), away=(), pinned=(), flops=0, nbytes=0):
    spec = pl.BlockSpec(memory_space=pltpu.VMEM)
    far = pl.BlockSpec(memory_space=pltpu.HBM)
    scratch, many = list(scratch), len(out)
    own = len(scratch)
    for i in away:
        scratch += [pltpu.VMEM(out[i].shape, out[i].dtype), pltpu.SemaphoreType.DMA]

    def run(*refs):
        outs, extra = list(refs[ins : ins + many]), refs[ins + many :]
        moves = []
        for n, i in enumerate(away):
            staged, sem = extra[own + 2 * n : own + 2 * n + 2]
            moves.append(pltpu.make_async_copy(staged, outs[i], sem))
            outs[i] = staged
        kernel(*refs[:ins], *outs, *extra[:own])
        for move in moves:
            move.start()
        for move in moves:
            move.wait()

    made = pl.pallas_call(
        run,
        out_shape=tuple(
            pltpu.HBM(o.shape, o.dtype) if i in away else pltpu.VMEM(o.shape, o.dtype) if i in pinned else o
            for i, o in enumerate(out)
        ),
        in_specs=[pl.BlockSpec(memory_space=pltpu.SMEM)] + [spec] * (ins - 1 - held) + [far] * held,
        out_specs=tuple(far if i in away else spec for i in range(many)),
        scratch_shapes=scratch,
        compiler_params=pltpu.CompilerParams(vmem_limit_bytes=16 * MIB),
        cost_estimate=pl.CostEstimate(flops=flops, bytes_accessed=nbytes, transcendentals=0),
    )
    near = ins - held
    return lambda *args: made(*args[:near], *(pltpu.with_memory_space_constraint(a, pltpu.HBM) for a in args[near:]))


def fetch(place, block, swapped, second, table, sems):
    core, half = place[0], place[1]
    count = block.shape[0]
    quarter = count // 4
    copies = [pltpu.make_async_copy(block, table.at[pl.ds(pl.multiple_of(half * count, count), count), :], sems.at[0])]
    for i, piece in enumerate(swapped):
        which = core if i < 2 else 1 - core
        at = pl.multiple_of((1 - half) * count + (2 * which + i % 2) * quarter, quarter)
        source = piece.at[pl.ds(second * quarter, quarter), :]
        copies.append(pltpu.make_async_copy(source, table.at[pl.ds(at, quarter), :], sems.at[1 + i]))
    for copy in copies:
        copy.start()
    return copies


def store(count, width):
    return [pltpu.VMEM((count, width), bf16), pltpu.SemaphoreType.DMA((5,))]


def row_squares(matrix):
    column = jnp.sum(jnp.square(matrix.astype(f32)), axis=1, keepdims=True)
    return jnp.broadcast_to(column, (matrix.shape[0], 128)).T[0:1]


def pack_kernel(place, given, marked, out, points, members, sems):
    copies = [pltpu.make_async_copy(given, points, sems.at[0]), pltpu.make_async_copy(marked, members, sems.at[1])]
    for copy in copies:
        copy.start()
    for copy in copies:
        copy.wait()
    rows, width = points.shape
    code = jnp.broadcast_to(members[...], (PACK, rows))
    row = lax.broadcasted_iota(i32, (PACK, rows), 0)
    digits = jnp.where(row == 0, code // DIGIT, jnp.where(row == 1, code % DIGIT, 0)).astype(f32).astype(bf16)
    lane = lax.broadcasted_iota(i32, (rows, width), 1) - place[3] * rows
    spot = jnp.where(lane == lax.broadcasted_iota(i32, (rows, width), 0), 1.0, 0.0).astype(bf16)
    tail = jnp.dot(digits, spot, preferred_element_type=f32).astype(bf16)
    for i in range(out.shape[0]):
        out[i, :rows, :] = points[...]
        out[i, rows:, :] = tail


def affinity_kernel(
    rows, place, came, own, up, down, up_o, down_o, kernel, keep, send, table, spread, arrival, anchors, sems
):
    first = pltpu.make_async_copy(came, spread, arrival)
    first.start()
    copies = fetch(place, own, (up, down, up_o, down_o), 0, anchors, sems)
    first.wait()
    core = place[0]
    ring, _, width = spread.shape
    half = keep.shape[0]
    count = anchors.shape[0]
    points = ring * rows
    codes = jnp.sum(spread[:, rows:, :].astype(f32), axis=0)
    members = (codes[0:1, :points] * DIGIT + codes[1:2, :points]).astype(i32)
    label = lax.broadcasted_iota(i32, (half, points), 0)
    for ref, part in ((keep, 0), (send, 1)):
        which = jnp.where(core == 0, part, 1 - part)
        hit = jnp.where(label + which * half == members, 1.0, 0.0)
        table[part * half : (part + 1) * half, :] = hit.astype(bf16)
        tally = jnp.sum(hit, axis=1, keepdims=True)
        big = jnp.floor(tally * (1.0 / DIGIT))
        lane = lax.broadcasted_iota(i32, (half, TALLY), 1)
        digits = jnp.where(lane == 0, big, jnp.where(lane == 1, tally - big * DIGIT, 0.0))
        ref[:, count:] = digits.astype(bf16)
    visitors = spread[:, :rows, :].reshape(points, width)
    length = lax.rsqrt(jnp.sum(jnp.square(visitors.astype(f32)), axis=1, keepdims=True) + epsilon) * math.sqrt(width)
    for copy in copies:
        copy.wait()
    tile = min(256, count)

    for at in range(0, count, tile):
        values = spread[:, :rows, :].reshape(points, width)
        marks = anchors[pl.ds(at, tile), :]
        factor = lax.rsqrt(row_squares(marks) + epsilon)
        part = jnp.exp(across(values, marks) * length * factor).astype(bf16)
        kernel[:, pl.ds(at, tile)] = part
        sums = jnp.dot(table[...], part, preferred_element_type=f32).astype(bf16)
        keep[:, pl.ds(at, tile)] = sums[:half]
        send[:, pl.ds(at, tile)] = sums[half:]


def project(place, kernel, maps, owners, rows, at, tile):
    spots = [pl.multiple_of(lax.bitwise_xor(place[3], d) * rows, rows) for d in owners]
    span = jnp.concatenate([kernel[pl.ds(spot, rows), :] for spot in spots])
    return jnp.dot(span, maps[:, pl.ds(at, tile)], preferred_element_type=f32)


def leave_kernel(rows, place, kernel, white, up, down, up_o, down_o, leave, token, maps, sems):
    copies = fetch(place, white, (up, down, up_o, down_o), 1, maps, sems)
    for copy in copies:
        copy.wait()
    token[...] = jnp.zeros_like(token)
    tile = min(256, leave.shape[1])
    for at in range(0, leave.shape[1], tile):
        leave[:, at : at + tile] = project(place, kernel, maps, LEAVE, rows, at, tile).astype(bf16)


def stay_kernel(rows, place, kernel, white, up, down, up_o, down_o, stay, maps, sems):
    for copy in fetch(place, white, (up, down, up_o, down_o), 1, maps, sems):
        copy.wait()
    tile = min(256, stay.shape[1])
    for at in range(0, stay.shape[1], tile):
        stay[:, at : at + tile] = project(place, kernel, maps, STAY, rows, at, tile).astype(bf16)


def merge_kernel(place, kept, arrived, keep, send, token):
    half = keep.shape[0]
    both = (kept[...].astype(f32) + arrived[...].astype(f32)).astype(bf16)
    keep[...] = both[:half]
    send[...] = both[half:]
    token[...] = jnp.zeros_like(token)


def cluster_kernel(place, spread, _, white, up, down, up_o, down_o, mapped, number, maps, sems):
    copies = fetch(place, white, (up, down, up_o, down_o), 1, maps, sems)
    count = maps.shape[0]
    share = spread.shape[1]
    total = jnp.sum(spread[...].astype(f32), axis=0)
    sums = total[:, :count]
    high = sums.astype(bf16).astype(f32)
    both = jnp.concatenate([high, sums - high]).astype(bf16)
    tally = total[:, count : count + 1] * DIGIT + total[:, count + 1 : count + 2]
    number[...] = jnp.broadcast_to(jnp.maximum(tally, 1.0), number.shape)
    for copy in copies:
        copy.wait()
    result = jnp.dot(both, maps[...], preferred_element_type=f32)
    mapped[...] = jnp.broadcast_to((result[:share] + result[share:])[None], mapped.shape)


def pair_kernel(place, keep, theirs, _, paired):
    paired[...] = (keep[...].astype(f32) + theirs[...].astype(f32)).astype(bf16)


def means_kernel(place, parts, number, _, sent):
    means = jnp.sum(parts[...], axis=0) / number[...]
    sent[...] = jnp.broadcast_to(means[None], sent.shape).astype(bf16)


def feature_kernel(place, owners, *rest):
    kept, last, features, again, choose = rest
    both = (kept[...].astype(f32) + last[...].astype(f32)).astype(bf16)
    features[...] = both
    again[...] = both
    slots, clusters = choose.shape
    owned = owners[...] == place[2]
    row = lax.broadcasted_iota(i32, (clusters, clusters), 0)
    col = lax.broadcasted_iota(i32, (clusters, clusters), 1)
    before = jnp.where(row < col, 1.0, 0.0).astype(bf16)
    mark = jnp.broadcast_to(jnp.where(owned, 1.0, 0.0), (slots, clusters))
    rank = jnp.dot(mark.astype(bf16), before, preferred_element_type=f32)
    slot = lax.broadcasted_iota(i32, (slots, clusters), 0).astype(f32)
    choose[...] = jnp.where(rank == slot, mark, 0.0).astype(bf16)


def after_kernel(place, means, _, same):
    same[...] = means[...]


def half_scores(features, means, choose, at):
    half = means.shape[0]
    norms = row_squares(means[...])
    scores = (norms - 2.0 * across(features[...], means[...])) * (1.0 / means.shape[1])
    owned = jnp.dot(choose[:, pl.ds(at, half)], means[...], preferred_element_type=f32)
    return scores, owned


def near_kernel(place, features, means, choose, scores, owned):
    half = means.shape[0]
    at = pl.multiple_of(place[0] * half, half)
    scores[...], owned[...] = half_scores(features, means, choose, at)


def far_kernel(place, features, means, choose, near_scores, near_owned, scores, owned):
    half = means.shape[0]
    there = pl.multiple_of((1 - place[0]) * half, half)
    here = pl.multiple_of(place[0] * half, half)
    far, rest = half_scores(features, means, choose, there)
    scores[:, pl.ds(there, half)] = far
    scores[:, pl.ds(here, half)] = near_scores[...]
    owned[...] = (near_owned[...] + rest).astype(bf16)


def body(points, membership, landmark_pool, landmark_ids, whitening, owner_map):
    rows, width = points.shape
    count, rank_width = whitening.shape
    clusters = owner_map.shape[0]
    ring = lax.axis_size("z")
    core = lax.axis_index("c")
    quarter = count // 4
    half = clusters // 2
    peers = math.prod(lax.axis_size(name) for name in PLANE)
    share = half // peers
    groups = lax.axis_size("yh") * lax.axis_size("x") * lax.axis_size("c")
    array = jax.ShapeDtypeStruct
    place = jnp.stack([core, lax.axis_index("yl"), lax.axis_index(("yh", "x", "c")), lax.axis_index("z")]).astype(i32)

    (block,) = call(
        pack_kernel,
        (array((ring, rows + PACK, width), bf16),),
        3,
        2,
        [pltpu.VMEM((rows, width), bf16), pltpu.VMEM((1, rows), i32), pltpu.SemaphoreType.DMA((2,))],
        away=(0,),
        nbytes=2 * MIB,
    )(place, points, membership.reshape(1, rows))
    spread = lax.all_to_all(block, "z", 0, 0)

    landmarks = landmark_pool[landmark_ids]

    def load(which):
        return jnp.concatenate(
            [lax.dynamic_slice_in_dim(m, which * quarter, quarter, 0) for m in (landmarks, whitening)]
        )

    up = hop(load(2 * core), ("yh", "yl"), 1)
    down = hop(load(2 * core + 1), ("yh", "yl"), -1)
    up_o, down_o = flip(up, "c", 1), flip(down, "c", 1)
    pieces = (up, down, up_o, down_o)

    kernel, keep, send = call(
        functools.partial(affinity_kernel, rows),
        (
            array((ring * rows, 2 * count), bf16),
            array((half, 2 * count + TALLY), bf16),
            array((half, 2 * count + TALLY), bf16),
        ),
        7,
        6,
        [
            pltpu.VMEM((clusters, ring * rows), bf16),
            pltpu.VMEM(spread.shape, bf16),
            pltpu.SemaphoreType.DMA,
            *store(2 * count, width),
        ],
        flops=2 * ring * rows * 2 * count * (width + clusters),
        nbytes=6 * MIB,
    )(place, spread, landmarks, *pieces)

    theirs = flip(send, "c", 1)
    token = array((8, 128), f32)

    leave, done = call(
        functools.partial(leave_kernel, rows),
        (array((ring // 2 * rows, rank_width), bf16), token),
        7,
        5,
        store(2 * count, rank_width),
        away=(0,),
        flops=ring * rows * 2 * count * rank_width,
        nbytes=3 * MIB,
    )(place, kernel, whitening, *pieces)
    (paired,) = call(pair_kernel, (array(keep.shape, bf16),), 4, away=(0,), nbytes=2 * MIB)(place, keep, theirs, done)
    gathered = lax.all_to_all(paired.reshape(peers, share, -1), PLANE, 0, 0)

    def merge(kept, leave, partner, work):
        size = array((kept.shape[0] // 2, rank_width), bf16)
        arrived = flip(leave, "z", partner)
        return call(merge_kernel, (size, size, token), 3, away=(0, 1), flops=work, nbytes=MIB)(place, kept, arrived)

    (stay,) = call(
        functools.partial(stay_kernel, rows),
        (array((ring // 2 * rows, rank_width), bf16),),
        7,
        5,
        store(2 * count, rank_width),
        flops=LONG,
        nbytes=3 * MIB,
    )(place, kernel, whitening, *pieces)
    kept, leave, done = merge(stay, leave, 1, 0)
    mapped, number = call(
        cluster_kernel,
        (array((ring, share, rank_width), f32), array((share, rank_width), f32)),
        8,
        5,
        store(2 * count, rank_width),
        away=(0,),
        flops=LONG,
        nbytes=3 * MIB,
    )(place, gathered, done, whitening, *pieces)
    over = lax.all_to_all(mapped, "z", 0, 0)
    kept, leave, done = merge(kept, leave, 3, LONG)
    (sent,) = call(means_kernel, (array((peers, share, rank_width), bf16),), 4, 1, away=(0,), nbytes=MIB)(
        place, over, number, done
    )
    mine = lax.all_to_all(sent, PLANE, 0, 0).reshape(half, rank_width)
    last = flip(leave, "z", 7)
    features, again, choose = call(
        feature_kernel,
        (
            array((rows, rank_width), bf16),
            array((rows, rank_width), bf16),
            array((clusters // groups, clusters), bf16),
        ),
        4,
        pinned=(1,),
        nbytes=2 * MIB,
    )(place, owner_map.reshape(1, clusters), kept, last)
    (mine,) = call(after_kernel, (array(mine.shape, bf16),), 3, nbytes=MIB)(place, mine, choose)
    other = flip(mine, "c", 1)
    near_scores, near_owned = call(
        near_kernel, (array((rows, half), f32), array((clusters // groups, rank_width), f32)), 4, nbytes=MIB
    )(place, again, mine, choose)
    scores, owned = call(
        far_kernel, (array((rows, clusters), f32), array((clusters // groups, rank_width), bf16)), 6, nbytes=MIB
    )(place, again, other, choose, near_scores, near_owned)
    return (features, owned, scores)


def build(mesh, factors):
    fine = Mesh(mesh.devices.reshape(factors), ALL)
    blk, dp = ("z", "yl"), ("yh", "x", "c")
    return jax.shard_map(
        body,
        mesh=fine,
        in_specs=(P(ALL, None), P(ALL), P(blk, None), P(blk), P(blk, None), P()),
        out_specs=(P(ALL, None), P(dp, None), P(ALL, None)),
        check_vma=False,
    )


def solution(mesh):
    return build(mesh, (4, 4, 2, 8, 2))
```

```python
import functools
import math

import jax
import jax.numpy as jnp
from jax import lax
from jax.experimental import pallas as pl
from jax.experimental.pallas import tpu as pltpu
from jax.sharding import Mesh, PartitionSpec as P

epsilon = 1e-06
bf16 = jnp.bfloat16
f32 = jnp.float32
i32 = jnp.int32
ALL = ("yh", "x", "c", "z", "yl")
PLANE = ("yh", "x", "yl")
PACK = 8
LONG = 1 << 36
LEAVE = (1, 6, 2, 5)
STAY = (0, 7, 3, 4)
DIGIT = 128
TALLY = 128
MIB = 1 << 20


def hop(value, axis, by):
    size = math.prod(lax.axis_size(name) for name in axis)
    return lax.ppermute(value, axis, [(i, (i + by) % size) for i in range(size)])


def flip(value, axis, bit):
    size = lax.axis_size(axis)
    return lax.ppermute(value, axis, [(i, i ^ bit) for i in range(size)])


def across(a, b):
    return lax.dot_general(a, b, (((1,), (1,)), ((), ())), preferred_element_type=f32)


def call(kernel, out, ins, held=0, scratch=(), away=(), pinned=(), flops=0, nbytes=0):
    spec = pl.BlockSpec(memory_space=pltpu.VMEM)
    far = pl.BlockSpec(memory_space=pltpu.HBM)
    scratch, many = list(scratch), len(out)
    own = len(scratch)
    for i in away:
        scratch += [pltpu.VMEM(out[i].shape, out[i].dtype), pltpu.SemaphoreType.DMA]

    def run(*refs):
        outs, extra = list(refs[ins : ins + many]), refs[ins + many :]
        moves = []
        for n, i in enumerate(away):
            staged, sem = extra[own + 2 * n : own + 2 * n + 2]
            moves.append(pltpu.make_async_copy(staged, outs[i], sem))
            outs[i] = staged
        kernel(*refs[:ins], *outs, *extra[:own])
        for move in moves:
            move.start()
        for move in moves:
            move.wait()

    made = pl.pallas_call(
        run,
        out_shape=tuple(
            pltpu.HBM(o.shape, o.dtype) if i in away else pltpu.VMEM(o.shape, o.dtype) if i in pinned else o
            for i, o in enumerate(out)
        ),
        in_specs=[pl.BlockSpec(memory_space=pltpu.SMEM)] + [spec] * (ins - 1 - held) + [far] * held,
        out_specs=tuple(far if i in away else spec for i in range(many)),
        scratch_shapes=scratch,
        compiler_params=pltpu.CompilerParams(vmem_limit_bytes=16 * MIB),
        cost_estimate=pl.CostEstimate(flops=flops, bytes_accessed=nbytes, transcendentals=0),
    )
    near = ins - held
    return lambda *args: made(*args[:near], *(pltpu.with_memory_space_constraint(a, pltpu.HBM) for a in args[near:]))


def fetch(place, block, swapped, second, table, sems):
    core, half = place[0], place[1]
    count = block.shape[0]
    quarter = count // 4
    copies = [pltpu.make_async_copy(block, table.at[pl.ds(pl.multiple_of(half * count, count), count), :], sems.at[0])]
    for i, piece in enumerate(swapped):
        which = core if i < 2 else 1 - core
        at = pl.multiple_of((1 - half) * count + (2 * which + i % 2) * quarter, quarter)
        source = piece.at[pl.ds(second * quarter, quarter), :]
        copies.append(pltpu.make_async_copy(source, table.at[pl.ds(at, quarter), :], sems.at[1 + i]))
    for copy in copies:
        copy.start()
    return copies


def store(count, width):
    return [pltpu.VMEM((count, width), bf16), pltpu.SemaphoreType.DMA((5,))]


def row_squares(matrix):
    column = jnp.sum(jnp.square(matrix.astype(f32)), axis=1, keepdims=True)
    return jnp.broadcast_to(column, (matrix.shape[0], 128)).T[0:1]


def pack_kernel(place, given, marked, out, points, members, sems):
    copies = [pltpu.make_async_copy(given, points, sems.at[0]), pltpu.make_async_copy(marked, members, sems.at[1])]
    for copy in copies:
        copy.start()
    for copy in copies:
        copy.wait()
    rows, width = points.shape
    code = jnp.broadcast_to(members[...], (PACK, rows))
    row = lax.broadcasted_iota(i32, (PACK, rows), 0)
    digits = jnp.where(row == 0, code // DIGIT, jnp.where(row == 1, code % DIGIT, 0)).astype(f32).astype(bf16)
    lane = lax.broadcasted_iota(i32, (rows, width), 1) - place[3] * rows
    spot = jnp.where(lane == lax.broadcasted_iota(i32, (rows, width), 0), 1.0, 0.0).astype(bf16)
    tail = jnp.dot(digits, spot, preferred_element_type=f32).astype(bf16)
    for i in range(out.shape[0]):
        out[i, :rows, :] = points[...]
        out[i, rows:, :] = tail


def affinity_kernel(
    rows, place, came, own, up, down, up_o, down_o, kernel, keep, send, table, spread, arrival, anchors, sems
):
    first = pltpu.make_async_copy(came, spread, arrival)
    first.start()
    copies = fetch(place, own, (up, down, up_o, down_o), 0, anchors, sems)
    first.wait()
    core = place[0]
    ring, _, width = spread.shape
    half = keep.shape[0]
    count = anchors.shape[0]
    points = ring * rows
    codes = jnp.sum(spread[:, rows:, :].astype(f32), axis=0)
    members = (codes[0:1, :points] * DIGIT + codes[1:2, :points]).astype(i32)
    label = lax.broadcasted_iota(i32, (half, points), 0)
    for ref, part in ((keep, 0), (send, 1)):
        which = jnp.where(core == 0, part, 1 - part)
        hit = jnp.where(label + which * half == members, 1.0, 0.0)
        table[part * half : (part + 1) * half, :] = hit.astype(bf16)
        tally = jnp.sum(hit, axis=1, keepdims=True)
        big = jnp.floor(tally * (1.0 / DIGIT))
        lane = lax.broadcasted_iota(i32, (half, TALLY), 1)
        digits = jnp.where(lane == 0, big, jnp.where(lane == 1, tally - big * DIGIT, 0.0))
        ref[:, count:] = digits.astype(bf16)
    visitors = spread[:, :rows, :].reshape(points, width)
    length = lax.rsqrt(jnp.sum(jnp.square(visitors.astype(f32)), axis=1, keepdims=True) + epsilon) * math.sqrt(width)
    for copy in copies:
        copy.wait()
    tile = min(256, count)

    for at in range(0, count, tile):
        values = spread[:, :rows, :].reshape(points, width)
        marks = anchors[pl.ds(at, tile), :]
        factor = lax.rsqrt(row_squares(marks) + epsilon)
        part = jnp.exp(across(values, marks) * length * factor).astype(bf16)
        kernel[:, pl.ds(at, tile)] = part
        sums = jnp.dot(table[...], part, preferred_element_type=f32).astype(bf16)
        keep[:, pl.ds(at, tile)] = sums[:half]
        send[:, pl.ds(at, tile)] = sums[half:]


def project(place, kernel, maps, owners, rows, at, tile):
    spots = [pl.multiple_of(lax.bitwise_xor(place[3], d) * rows, rows) for d in owners]
    span = jnp.concatenate([kernel[pl.ds(spot, rows), :] for spot in spots])
    return jnp.dot(span, maps[:, pl.ds(at, tile)], preferred_element_type=f32)


def leave_kernel(rows, place, kernel, white, up, down, up_o, down_o, leave, token, maps, sems):
    copies = fetch(place, white, (up, down, up_o, down_o), 1, maps, sems)
    for copy in copies:
        copy.wait()
    token[...] = jnp.zeros_like(token)
    tile = min(256, leave.shape[1])
    for at in range(0, leave.shape[1], tile):
        leave[:, at : at + tile] = project(place, kernel, maps, LEAVE, rows, at, tile).astype(bf16)


def stay_kernel(rows, place, kernel, white, up, down, up_o, down_o, stay, maps, sems):
    for copy in fetch(place, white, (up, down, up_o, down_o), 1, maps, sems):
        copy.wait()
    tile = min(256, stay.shape[1])
    for at in range(0, stay.shape[1], tile):
        stay[:, at : at + tile] = project(place, kernel, maps, STAY, rows, at, tile).astype(bf16)


def merge_kernel(place, kept, arrived, keep, send, token):
    half = keep.shape[0]
    both = (kept[...].astype(f32) + arrived[...].astype(f32)).astype(bf16)
    keep[...] = both[:half]
    send[...] = both[half:]
    token[...] = jnp.zeros_like(token)


def cluster_kernel(place, spread, _, white, up, down, up_o, down_o, mapped, number, maps, sems):
    copies = fetch(place, white, (up, down, up_o, down_o), 1, maps, sems)
    count = maps.shape[0]
    share = spread.shape[1]
    total = jnp.sum(spread[...].astype(f32), axis=0)
    sums = total[:, :count]
    high = sums.astype(bf16).astype(f32)
    both = jnp.concatenate([high, sums - high]).astype(bf16)
    tally = total[:, count : count + 1] * DIGIT + total[:, count + 1 : count + 2]
    number[...] = jnp.broadcast_to(jnp.maximum(tally, 1.0), number.shape)
    for copy in copies:
        copy.wait()
    result = jnp.dot(both, maps[...], preferred_element_type=f32)
    mapped[...] = jnp.broadcast_to((result[:share] + result[share:])[None], mapped.shape).astype(bf16)


def pair_kernel(place, keep, theirs, _, paired):
    paired[...] = (keep[...].astype(f32) + theirs[...].astype(f32)).astype(bf16)


def means_kernel(place, parts, number, _, sent):
    means = jnp.sum(parts[...].astype(f32), axis=0) / number[...]
    sent[...] = jnp.broadcast_to(means[None], sent.shape).astype(bf16)


def feature_kernel(place, owners, *rest):
    kept, last, features, again, choose = rest
    both = (kept[...].astype(f32) + last[...].astype(f32)).astype(bf16)
    features[...] = both
    again[...] = both
    slots, clusters = choose.shape
    owned = owners[...] == place[2]
    row = lax.broadcasted_iota(i32, (clusters, clusters), 0)
    col = lax.broadcasted_iota(i32, (clusters, clusters), 1)
    before = jnp.where(row < col, 1.0, 0.0).astype(bf16)
    mark = jnp.broadcast_to(jnp.where(owned, 1.0, 0.0), (slots, clusters))
    rank = jnp.dot(mark.astype(bf16), before, preferred_element_type=f32)
    slot = lax.broadcasted_iota(i32, (slots, clusters), 0).astype(f32)
    choose[...] = jnp.where(rank == slot, mark, 0.0).astype(bf16)


def after_kernel(place, means, _, same):
    same[...] = means[...]


def half_scores(features, means, choose, at):
    half = means.shape[0]
    norms = row_squares(means[...])
    scores = (norms - 2.0 * across(features[...], means[...])) * (1.0 / means.shape[1])
    owned = jnp.dot(choose[:, pl.ds(at, half)], means[...], preferred_element_type=f32)
    return scores, owned


def near_kernel(place, features, means, choose, scores, owned):
    half = means.shape[0]
    at = pl.multiple_of(place[0] * half, half)
    scores[...], owned[...] = half_scores(features, means, choose, at)


def far_kernel(place, features, means, choose, near_scores, near_owned, scores, owned):
    half = means.shape[0]
    there = pl.multiple_of((1 - place[0]) * half, half)
    here = pl.multiple_of(place[0] * half, half)
    far, rest = half_scores(features, means, choose, there)
    scores[:, pl.ds(there, half)] = far
    scores[:, pl.ds(here, half)] = near_scores[...]
    owned[...] = (near_owned[...] + rest).astype(bf16)


def body(points, membership, landmark_pool, landmark_ids, whitening, owner_map):
    rows, width = points.shape
    count, rank_width = whitening.shape
    clusters = owner_map.shape[0]
    ring = lax.axis_size("z")
    core = lax.axis_index("c")
    quarter = count // 4
    half = clusters // 2
    peers = math.prod(lax.axis_size(name) for name in PLANE)
    share = half // peers
    groups = lax.axis_size("yh") * lax.axis_size("x") * lax.axis_size("c")
    array = jax.ShapeDtypeStruct
    place = jnp.stack([core, lax.axis_index("yl"), lax.axis_index(("yh", "x", "c")), lax.axis_index("z")]).astype(i32)

    (block,) = call(
        pack_kernel,
        (array((ring, rows + PACK, width), bf16),),
        3,
        2,
        [pltpu.VMEM((rows, width), bf16), pltpu.VMEM((1, rows), i32), pltpu.SemaphoreType.DMA((2,))],
        away=(0,),
        nbytes=2 * MIB,
    )(place, points, membership.reshape(1, rows))
    spread = lax.all_to_all(block, "z", 0, 0)

    landmarks = landmark_pool[landmark_ids]

    def load(which):
        return jnp.concatenate(
            [lax.dynamic_slice_in_dim(m, which * quarter, quarter, 0) for m in (landmarks, whitening)]
        )

    up = hop(load(2 * core), ("yh", "yl"), 1)
    down = hop(load(2 * core + 1), ("yh", "yl"), -1)
    up_o, down_o = flip(up, "c", 1), flip(down, "c", 1)
    pieces = (up, down, up_o, down_o)

    kernel, keep, send = call(
        functools.partial(affinity_kernel, rows),
        (
            array((ring * rows, 2 * count), bf16),
            array((half, 2 * count + TALLY), bf16),
            array((half, 2 * count + TALLY), bf16),
        ),
        7,
        6,
        [
            pltpu.VMEM((clusters, ring * rows), bf16),
            pltpu.VMEM(spread.shape, bf16),
            pltpu.SemaphoreType.DMA,
            *store(2 * count, width),
        ],
        flops=2 * ring * rows * 2 * count * (width + clusters),
        nbytes=6 * MIB,
    )(place, spread, landmarks, *pieces)

    theirs = flip(send, "c", 1)
    token = array((8, 128), f32)

    leave, done = call(
        functools.partial(leave_kernel, rows),
        (array((ring // 2 * rows, rank_width), bf16), token),
        7,
        5,
        store(2 * count, rank_width),
        away=(0,),
        flops=ring * rows * 2 * count * rank_width,
        nbytes=3 * MIB,
    )(place, kernel, whitening, *pieces)
    (paired,) = call(pair_kernel, (array(keep.shape, bf16),), 4, away=(0,), nbytes=2 * MIB)(place, keep, theirs, done)
    gathered = lax.all_to_all(paired.reshape(peers, share, -1), PLANE, 0, 0)

    def merge(kept, leave, partner, work):
        size = array((kept.shape[0] // 2, rank_width), bf16)
        arrived = flip(leave, "z", partner)
        return call(merge_kernel, (size, size, token), 3, away=(0, 1), flops=work, nbytes=MIB)(place, kept, arrived)

    (stay,) = call(
        functools.partial(stay_kernel, rows),
        (array((ring // 2 * rows, rank_width), bf16),),
        7,
        5,
        store(2 * count, rank_width),
        flops=LONG,
        nbytes=3 * MIB,
    )(place, kernel, whitening, *pieces)
    kept, leave, done = merge(stay, leave, 1, 0)
    mapped, number = call(
        cluster_kernel,
        (array((ring, share, rank_width), bf16), array((share, rank_width), f32)),
        8,
        5,
        store(2 * count, rank_width),
        away=(0,),
        flops=LONG,
        nbytes=3 * MIB,
    )(place, gathered, done, whitening, *pieces)
    over = lax.all_to_all(mapped, "z", 0, 0)
    kept, leave, done = merge(kept, leave, 3, LONG)
    (sent,) = call(means_kernel, (array((peers, share, rank_width), bf16),), 4, 1, away=(0,), nbytes=MIB)(
        place, over, number, done
    )
    mine = lax.all_to_all(sent, PLANE, 0, 0).reshape(half, rank_width)
    last = flip(leave, "z", 7)
    features, again, choose = call(
        feature_kernel,
        (
            array((rows, rank_width), bf16),
            array((rows, rank_width), bf16),
            array((clusters // groups, clusters), bf16),
        ),
        4,
        pinned=(1,),
        nbytes=2 * MIB,
    )(place, owner_map.reshape(1, clusters), kept, last)
    (mine,) = call(after_kernel, (array(mine.shape, bf16),), 3, nbytes=MIB)(place, mine, choose)
    other = flip(mine, "c", 1)
    near_scores, near_owned = call(
        near_kernel, (array((rows, half), f32), array((clusters // groups, rank_width), f32)), 4, nbytes=MIB
    )(place, again, mine, choose)
    scores, owned = call(
        far_kernel, (array((rows, clusters), f32), array((clusters // groups, rank_width), bf16)), 6, nbytes=MIB
    )(place, again, other, choose, near_scores, near_owned)
    return (features, owned, scores)


def build(mesh, factors):
    fine = Mesh(mesh.devices.reshape(factors), ALL)
    blk, dp = ("z", "yl"), ("yh", "x", "c")
    return jax.shard_map(
        body,
        mesh=fine,
        in_specs=(P(ALL, None), P(ALL), P(blk, None), P(blk), P(blk, None), P()),
        out_specs=(P(ALL, None), P(dp, None), P(ALL, None)),
        check_vma=False,
    )


def solution(mesh):
    return build(mesh, (4, 4, 2, 8, 2))
```

```python
import functools
import math

import jax
import jax.numpy as jnp
from jax import lax
from jax.experimental import pallas as pl
from jax.experimental.pallas import tpu as pltpu
from jax.sharding import Mesh, PartitionSpec as P

epsilon = 1e-06
bf16 = jnp.bfloat16
f32 = jnp.float32
i32 = jnp.int32
ALL = ("yh", "x", "c", "z", "yl")
PLANE = ("yh", "x", "yl")
PACK = 8
LONG = 1 << 36
LEAVE = (1, 6, 2, 5)
STAY = (0, 7, 3, 4)
DIGIT = 128
TALLY = 128
MIB = 1 << 20


def hop(value, axis, by):
    size = math.prod(lax.axis_size(name) for name in axis)
    return lax.ppermute(value, axis, [(i, (i + by) % size) for i in range(size)])


def flip(value, axis, bit):
    size = lax.axis_size(axis)
    return lax.ppermute(value, axis, [(i, i ^ bit) for i in range(size)])


def across(a, b):
    return lax.dot_general(a, b, (((1,), (1,)), ((), ())), preferred_element_type=f32)


def call(kernel, out, ins, held=0, scratch=(), away=(), pinned=(), flops=0, nbytes=0):
    spec = pl.BlockSpec(memory_space=pltpu.VMEM)
    far = pl.BlockSpec(memory_space=pltpu.HBM)
    scratch, many = list(scratch), len(out)
    own = len(scratch)
    for i in away:
        scratch += [pltpu.VMEM(out[i].shape, out[i].dtype), pltpu.SemaphoreType.DMA]

    def run(*refs):
        outs, extra = list(refs[ins : ins + many]), refs[ins + many :]
        moves = []
        for n, i in enumerate(away):
            staged, sem = extra[own + 2 * n : own + 2 * n + 2]
            moves.append(pltpu.make_async_copy(staged, outs[i], sem))
            outs[i] = staged
        kernel(*refs[:ins], *outs, *extra[:own])
        for move in moves:
            move.start()
        for move in moves:
            move.wait()

    made = pl.pallas_call(
        run,
        out_shape=tuple(
            pltpu.HBM(o.shape, o.dtype) if i in away else pltpu.VMEM(o.shape, o.dtype) if i in pinned else o
            for i, o in enumerate(out)
        ),
        in_specs=[pl.BlockSpec(memory_space=pltpu.SMEM)] + [spec] * (ins - 1 - held) + [far] * held,
        out_specs=tuple(far if i in away else spec for i in range(many)),
        scratch_shapes=scratch,
        compiler_params=pltpu.CompilerParams(vmem_limit_bytes=16 * MIB),
        cost_estimate=pl.CostEstimate(flops=flops, bytes_accessed=nbytes, transcendentals=0),
    )
    near = ins - held
    return lambda *args: made(*args[:near], *(pltpu.with_memory_space_constraint(a, pltpu.HBM) for a in args[near:]))


def fetch(place, block, swapped, second, table, sems):
    core, half = place[0], place[1]
    count = block.shape[0]
    quarter = count // 4
    copies = [pltpu.make_async_copy(block, table.at[pl.ds(pl.multiple_of(half * count, count), count), :], sems.at[0])]
    for i, piece in enumerate(swapped):
        which = core if i < 2 else 1 - core
        at = pl.multiple_of((1 - half) * count + (2 * which + i % 2) * quarter, quarter)
        source = piece.at[pl.ds(second * quarter, quarter), :]
        copies.append(pltpu.make_async_copy(source, table.at[pl.ds(at, quarter), :], sems.at[1 + i]))
    for copy in copies:
        copy.start()
    return copies


def store(count, width):
    return [pltpu.VMEM((count, width), bf16), pltpu.SemaphoreType.DMA((5,))]


def row_squares(matrix):
    column = jnp.sum(jnp.square(matrix.astype(f32)), axis=1, keepdims=True)
    return jnp.broadcast_to(column, (matrix.shape[0], 128)).T[0:1]


def pack_kernel(place, given, marked, out, points, members, sems):
    copies = [pltpu.make_async_copy(given, points, sems.at[0]), pltpu.make_async_copy(marked, members, sems.at[1])]
    for copy in copies:
        copy.start()
    for copy in copies:
        copy.wait()
    rows, width = points.shape
    code = jnp.broadcast_to(members[...], (PACK, rows))
    row = lax.broadcasted_iota(i32, (PACK, rows), 0)
    digits = jnp.where(row == 0, code // DIGIT, jnp.where(row == 1, code % DIGIT, 0)).astype(f32).astype(bf16)
    lane = lax.broadcasted_iota(i32, (rows, width), 1) - place[3] * rows
    spot = jnp.where(lane == lax.broadcasted_iota(i32, (rows, width), 0), 1.0, 0.0).astype(bf16)
    tail = jnp.dot(digits, spot, preferred_element_type=f32).astype(bf16)
    for i in range(out.shape[0]):
        out[i, :rows, :] = points[...]
        out[i, rows:, :] = tail


def affinity_kernel(
    rows, place, came, own, up, down, up_o, down_o, kernel, keep, send, table, spread, arrival, anchors, sems
):
    first = pltpu.make_async_copy(came, spread, arrival)
    first.start()
    copies = fetch(place, own, (up, down, up_o, down_o), 0, anchors, sems)
    first.wait()
    core = place[0]
    ring, _, width = spread.shape
    half = keep.shape[0]
    count = anchors.shape[0]
    points = ring * rows
    codes = jnp.sum(spread[:, rows:, :].astype(f32), axis=0)
    members = (codes[0:1, :points] * DIGIT + codes[1:2, :points]).astype(i32)
    label = lax.broadcasted_iota(i32, (half, points), 0)
    for ref, part in ((keep, 0), (send, 1)):
        which = jnp.where(core == 0, part, 1 - part)
        hit = jnp.where(label + which * half == members, 1.0, 0.0)
        table[part * half : (part + 1) * half, :] = hit.astype(bf16)
        tally = jnp.sum(hit, axis=1, keepdims=True)
        big = jnp.floor(tally * (1.0 / DIGIT))
        lane = lax.broadcasted_iota(i32, (half, TALLY), 1)
        digits = jnp.where(lane == 0, big, jnp.where(lane == 1, tally - big * DIGIT, 0.0))
        ref[:, count:] = digits.astype(bf16)
    visitors = spread[:, :rows, :].reshape(points, width)
    length = lax.rsqrt(jnp.sum(jnp.square(visitors.astype(f32)), axis=1, keepdims=True) + epsilon) * math.sqrt(width)
    for copy in copies:
        copy.wait()
    tile = min(512, count)

    for at in range(0, count, tile):
        values = spread[:, :rows, :].reshape(points, width)
        marks = anchors[pl.ds(at, tile), :]
        factor = lax.rsqrt(row_squares(marks) + epsilon)
        part = jnp.exp(across(values, marks) * length * factor).astype(bf16)
        kernel[:, pl.ds(at, tile)] = part
        sums = jnp.dot(table[...], part, preferred_element_type=f32).astype(bf16)
        keep[:, pl.ds(at, tile)] = sums[:half]
        send[:, pl.ds(at, tile)] = sums[half:]


def project(place, kernel, maps, owners, rows, at, tile):
    spots = [pl.multiple_of(lax.bitwise_xor(place[3], d) * rows, rows) for d in owners]
    span = jnp.concatenate([kernel[pl.ds(spot, rows), :] for spot in spots])
    return jnp.dot(span, maps[:, pl.ds(at, tile)], preferred_element_type=f32)


def leave_kernel(rows, place, kernel, white, up, down, up_o, down_o, leave, token, maps, sems):
    copies = fetch(place, white, (up, down, up_o, down_o), 1, maps, sems)
    for copy in copies:
        copy.wait()
    token[...] = jnp.zeros_like(token)
    tile = min(512, leave.shape[1])
    for at in range(0, leave.shape[1], tile):
        leave[:, at : at + tile] = project(place, kernel, maps, LEAVE, rows, at, tile).astype(bf16)


def stay_kernel(rows, place, kernel, white, up, down, up_o, down_o, stay, maps, sems):
    for copy in fetch(place, white, (up, down, up_o, down_o), 1, maps, sems):
        copy.wait()
    tile = min(256, stay.shape[1])
    for at in range(0, stay.shape[1], tile):
        stay[:, at : at + tile] = project(place, kernel, maps, STAY, rows, at, tile).astype(bf16)


def merge_kernel(place, kept, arrived, keep, send, token):
    half = keep.shape[0]
    both = (kept[...].astype(f32) + arrived[...].astype(f32)).astype(bf16)
    keep[...] = both[:half]
    send[...] = both[half:]
    token[...] = jnp.zeros_like(token)


def cluster_kernel(place, spread, _, white, up, down, up_o, down_o, mapped, number, maps, sems):
    copies = fetch(place, white, (up, down, up_o, down_o), 1, maps, sems)
    count = maps.shape[0]
    share = spread.shape[1]
    total = jnp.sum(spread[...].astype(f32), axis=0)
    sums = total[:, :count]
    high = sums.astype(bf16).astype(f32)
    both = jnp.concatenate([high, sums - high]).astype(bf16)
    tally = total[:, count : count + 1] * DIGIT + total[:, count + 1 : count + 2]
    number[...] = jnp.broadcast_to(jnp.maximum(tally, 1.0), number.shape)
    for copy in copies:
        copy.wait()
    result = jnp.dot(both, maps[...], preferred_element_type=f32)
    mapped[...] = jnp.broadcast_to((result[:share] + result[share:])[None], mapped.shape).astype(bf16)


def pair_kernel(place, keep, theirs, _, paired):
    paired[...] = (keep[...].astype(f32) + theirs[...].astype(f32)).astype(bf16)


def means_kernel(place, parts, number, _, sent):
    means = jnp.sum(parts[...].astype(f32), axis=0) / number[...]
    sent[...] = jnp.broadcast_to(means[None], sent.shape).astype(bf16)


def feature_kernel(place, owners, *rest):
    kept, last, features, again, choose = rest
    both = (kept[...].astype(f32) + last[...].astype(f32)).astype(bf16)
    features[...] = both
    again[...] = both
    slots, clusters = choose.shape
    owned = owners[...] == place[2]
    row = lax.broadcasted_iota(i32, (clusters, clusters), 0)
    col = lax.broadcasted_iota(i32, (clusters, clusters), 1)
    before = jnp.where(row < col, 1.0, 0.0).astype(bf16)
    mark = jnp.broadcast_to(jnp.where(owned, 1.0, 0.0), (slots, clusters))
    rank = jnp.dot(mark.astype(bf16), before, preferred_element_type=f32)
    slot = lax.broadcasted_iota(i32, (slots, clusters), 0).astype(f32)
    choose[...] = jnp.where(rank == slot, mark, 0.0).astype(bf16)


def after_kernel(place, means, _, same):
    same[...] = means[...]


def half_scores(features, means, choose, at):
    half = means.shape[0]
    norms = row_squares(means[...])
    scores = (norms - 2.0 * across(features[...], means[...])) * (1.0 / means.shape[1])
    owned = jnp.dot(choose[:, pl.ds(at, half)], means[...], preferred_element_type=f32)
    return scores, owned


def near_kernel(place, features, means, choose, scores, owned):
    half = means.shape[0]
    at = pl.multiple_of(place[0] * half, half)
    scores[...], owned[...] = half_scores(features, means, choose, at)


def far_kernel(place, features, means, choose, near_scores, near_owned, scores, owned):
    half = means.shape[0]
    there = pl.multiple_of((1 - place[0]) * half, half)
    here = pl.multiple_of(place[0] * half, half)
    far, rest = half_scores(features, means, choose, there)
    scores[:, pl.ds(there, half)] = far
    scores[:, pl.ds(here, half)] = near_scores[...]
    owned[...] = (near_owned[...] + rest).astype(bf16)


def body(points, membership, landmark_pool, landmark_ids, whitening, owner_map):
    rows, width = points.shape
    count, rank_width = whitening.shape
    clusters = owner_map.shape[0]
    ring = lax.axis_size("z")
    core = lax.axis_index("c")
    quarter = count // 4
    half = clusters // 2
    peers = math.prod(lax.axis_size(name) for name in PLANE)
    share = half // peers
    groups = lax.axis_size("yh") * lax.axis_size("x") * lax.axis_size("c")
    array = jax.ShapeDtypeStruct
    place = jnp.stack([core, lax.axis_index("yl"), lax.axis_index(("yh", "x", "c")), lax.axis_index("z")]).astype(i32)

    (block,) = call(
        pack_kernel,
        (array((ring, rows + PACK, width), bf16),),
        3,
        2,
        [pltpu.VMEM((rows, width), bf16), pltpu.VMEM((1, rows), i32), pltpu.SemaphoreType.DMA((2,))],
        away=(0,),
        nbytes=2 * MIB,
    )(place, points, membership.reshape(1, rows))
    spread = lax.all_to_all(block, "z", 0, 0)

    landmarks = landmark_pool[landmark_ids]

    def load(which):
        return jnp.concatenate(
            [lax.dynamic_slice_in_dim(m, which * quarter, quarter, 0) for m in (landmarks, whitening)]
        )

    up = hop(load(2 * core), ("yh", "yl"), 1)
    down = hop(load(2 * core + 1), ("yh", "yl"), -1)
    up_o, down_o = flip(up, "c", 1), flip(down, "c", 1)
    pieces = (up, down, up_o, down_o)

    kernel, keep, send = call(
        functools.partial(affinity_kernel, rows),
        (
            array((ring * rows, 2 * count), bf16),
            array((half, 2 * count + TALLY), bf16),
            array((half, 2 * count + TALLY), bf16),
        ),
        7,
        6,
        [
            pltpu.VMEM((clusters, ring * rows), bf16),
            pltpu.VMEM(spread.shape, bf16),
            pltpu.SemaphoreType.DMA,
            *store(2 * count, width),
        ],
        flops=2 * ring * rows * 2 * count * (width + clusters),
        nbytes=6 * MIB,
    )(place, spread, landmarks, *pieces)

    theirs = flip(send, "c", 1)
    token = array((8, 128), f32)

    leave, done = call(
        functools.partial(leave_kernel, rows),
        (array((ring // 2 * rows, rank_width), bf16), token),
        7,
        5,
        store(2 * count, rank_width),
        away=(0,),
        flops=ring * rows * 2 * count * rank_width,
        nbytes=3 * MIB,
    )(place, kernel, whitening, *pieces)
    (paired,) = call(pair_kernel, (array(keep.shape, bf16),), 4, away=(0,), nbytes=2 * MIB)(place, keep, theirs, done)
    gathered = lax.all_to_all(paired.reshape(peers, share, -1), PLANE, 0, 0)

    def merge(kept, leave, partner, work):
        size = array((kept.shape[0] // 2, rank_width), bf16)
        arrived = flip(leave, "z", partner)
        return call(merge_kernel, (size, size, token), 3, away=(0, 1), flops=work, nbytes=MIB)(place, kept, arrived)

    (stay,) = call(
        functools.partial(stay_kernel, rows),
        (array((ring // 2 * rows, rank_width), bf16),),
        7,
        5,
        store(2 * count, rank_width),
        flops=LONG,
        nbytes=3 * MIB,
    )(place, kernel, whitening, *pieces)
    kept, leave, done = merge(stay, leave, 1, 0)
    mapped, number = call(
        cluster_kernel,
        (array((ring, share, rank_width), bf16), array((share, rank_width), f32)),
        8,
        5,
        store(2 * count, rank_width),
        away=(0,),
        flops=LONG,
        nbytes=3 * MIB,
    )(place, gathered, done, whitening, *pieces)
    over = lax.all_to_all(mapped, "z", 0, 0)
    kept, leave, done = merge(kept, leave, 3, LONG)
    (sent,) = call(means_kernel, (array((peers, share, rank_width), bf16),), 4, 1, away=(0,), nbytes=MIB)(
        place, over, number, done
    )
    mine = lax.all_to_all(sent, PLANE, 0, 0).reshape(half, rank_width)
    last = flip(leave, "z", 7)
    features, again, choose = call(
        feature_kernel,
        (
            array((rows, rank_width), bf16),
            array((rows, rank_width), bf16),
            array((clusters // groups, clusters), bf16),
        ),
        4,
        pinned=(1,),
        nbytes=2 * MIB,
    )(place, owner_map.reshape(1, clusters), kept, last)
    (mine,) = call(after_kernel, (array(mine.shape, bf16),), 3, nbytes=MIB)(place, mine, choose)
    other = flip(mine, "c", 1)
    near_scores, near_owned = call(
        near_kernel, (array((rows, half), f32), array((clusters // groups, rank_width), f32)), 4, nbytes=MIB
    )(place, again, mine, choose)
    scores, owned = call(
        far_kernel, (array((rows, clusters), f32), array((clusters // groups, rank_width), bf16)), 6, nbytes=MIB
    )(place, again, other, choose, near_scores, near_owned)
    return (features, owned, scores)


def build(mesh, factors):
    fine = Mesh(mesh.devices.reshape(factors), ALL)
    blk, dp = ("z", "yl"), ("yh", "x", "c")
    return jax.shard_map(
        body,
        mesh=fine,
        in_specs=(P(ALL, None), P(ALL), P(blk, None), P(blk), P(blk, None), P()),
        out_specs=(P(ALL, None), P(dp, None), P(ALL, None)),
        check_vma=False,
    )


def solution(mesh):
    return build(mesh, (4, 4, 2, 8, 2))
```
